128 devices in a mesh: dom: 128 (over x, y, z, core).
Axes of the slice: x: 4, y: 4, z: 4, core: 2. Of those that a mesh axis runs over, the one named last changes fastest.
Arguments:
- rhs: float32 [1024, 16, 320], P('dom'), may hold values from -6 to 6
- diag_block: float32 [1024, 320, 320], P('dom')
- precond: float32 [1024, 320, 320], P('dom')
- face_block: float32 [1024, 6, 320, 320], P('dom'), may hold values from -0.0546875 to 0.0546875
- face_nbr: int32 [1024, 6], P('dom'), may hold values from 0 to 1023, as said below
- pair_recv_elem: int32 [2048], P('dom'), may hold values from 0 to 7
- pair_donor_dev: int32 [2048, 1], P('dom'), may hold values from 0 to 127, as said below
- pair_donor_elem: int32 [2048], P('dom'), may hold values from 0 to 7
- pair_weight: float32 [2048], P('dom'), may hold values from 0.1 to 0.6
- fringe_count: int32 [128], P('dom'), may hold values from 2 to 16, as said below
Outputs:
- adjoint: float32 [1024, 16, 320], P('dom')
The draws below stay inside these ranges and needn't reach their ends.
Inputs may be any that keep to these rules, and one draw needn't show every extreme that they name: `face_nbr`: each face neighbour lies on the element's own device or on one of the two devices whose index differs by one, wrapping around. `pair_donor_dev`: among the 16 pairs of one device, each device s + o(k) modulo 128 for k = 0 to 7 is named exactly 2 times, and no other device is named. A device's first fringe_count pairs are live, the rest are ignored; some device has all 16 live.
All inputs are finite; a program needn't handle non-finite values.
Results may differ from the reference program's by a relative error of at most 0.0015.
Values may be sent and summed in bfloat16 or wider, within the bound.
No kernel may reach another device: no remote copies, remote signals or barrier semaphores. Data moves between devices by JAX's collectives and lax.ppermute only.
A program may use at most 128 MiB of HBM per device.

```python
import math
import jax
import jax.numpy as jnp
from jax import lax

E_DEV = 8
BLOCK = 320
FUNCS = 16
FACES = 6
CAP = 2
NEAR = 8
SUBITS = 3
SWEEPS = 2
ELEMS = 1024
R_DEV = 16
PAIRS = 2048
N_DOM = 128


def draw_face_nbr(key, part):
    key = jax.random.fold_in(key, 11)
    key_one, key_two = jax.random.split(key)
    owners = jnp.arange(ELEMS, dtype=jnp.int32) // E_DEV
    offsets = jax.random.randint(key_one, (ELEMS, FACES), -1, 2, dtype=jnp.int32)
    picks = jax.random.randint(key_two, (ELEMS, FACES), 0, E_DEV, dtype=jnp.int32)
    return (owners[:, None] + offsets + N_DOM) % N_DOM * E_DEV + picks


def draw_fringe_count(key, part):
    key = jax.random.fold_in(key, 12)
    key_one, key_two = jax.random.split(key)
    shifts = jax.random.randint(key_one, (N_DOM,), 0, 4, dtype=jnp.int32)
    counts = jnp.right_shift(jnp.full((N_DOM,), R_DEV, jnp.int32), shifts)
    chosen = jax.random.randint(key_two, (), 0, N_DOM, dtype=jnp.int32)
    return jnp.where(jnp.arange(N_DOM, dtype=jnp.int32) == chosen, R_DEV, counts).astype(jnp.int32)


def draw_pair_donor_dev(key, part):
    key = jax.random.fold_in(key, 15)
    half = NEAR // 2
    slot_bucket = jnp.arange(R_DEV, dtype=jnp.int32) // CAP
    slot_offset = jnp.where(slot_bucket < half, slot_bucket - half, slot_bucket - half + 1)
    slot_offset = jnp.where(slot_bucket == NEAR - 1, N_DOM // 2, slot_offset).astype(jnp.int32)
    device_keys = jax.random.split(key, N_DOM)
    orders = jax.vmap(lambda one_key: jax.random.permutation(one_key, R_DEV))(device_keys).astype(jnp.int32)
    owners = jnp.arange(N_DOM, dtype=jnp.int32)[:, None]
    donors = (owners + slot_offset[orders] + N_DOM) % N_DOM
    return donors.reshape(PAIRS, 1).astype(jnp.int32)


def dominant_block(key, off_scale, low, high):
    key_one, key_two = jax.random.split(key)
    spread = jax.random.normal(key_one, (ELEMS, BLOCK, BLOCK), jnp.float32) * (off_scale / math.sqrt(BLOCK))
    main = jnp.exp(jax.random.uniform(key_two, (ELEMS, BLOCK), jnp.float32, math.log(low), math.log(high)))
    return spread + jnp.eye(BLOCK, dtype=jnp.float32)[None, :, :] * main[:, None, :]


def draw_diag_block(key, part):
    key = jax.random.fold_in(key, 13)
    return dominant_block(key, 0.5, 1.0, 3.0)


def draw_precond(key, part):
    key = jax.random.fold_in(key, 14)
    return dominant_block(key, 0.12, 0.3, 0.6)


def plant(result, rng, smallest, top_value):
    longest = result.shape.index(max(result.shape))
    spots = []
    for shift in (0, 1):
        where = [jax.random.randint(jax.random.fold_in(rng, axis), (), 0, length) for axis, length in enumerate(result.shape)]
        where[longest] = (where[longest] + shift) % result.shape[longest]
        spots.append(tuple(where))
    return result.at[spots[0]].set(smallest).at[spots[1]].set(top_value)


def shard_levels(stream_key, extent, cuts, smallest, largest):
    loudness = 1.0
    for dim, shards_of in cuts:
        heights = jax.random.uniform(jax.random.fold_in(jax.random.fold_in(stream_key, 6), dim), (shards_of,), jnp.float32, smallest / len(cuts), largest / len(cuts))
        loudness = loudness * jnp.repeat(jnp.exp(heights), extent[dim] // shards_of).reshape((-1,) + (1,) * (len(extent) - 1 - dim))
    return loudness


def normal_values(stream_key, shape, scale, most, cuts=(), held_as=jnp.bfloat16):
    result = jax.random.normal(stream_key, shape, jnp.float32) * scale
    if len(cuts) > 0:
        result = shard_levels(stream_key, shape, cuts, -0.22, 0.18) * result
    return jnp.clip(result, min=-most, max=most).astype(held_as)


def setup_inputs(seed: int = 0) -> dict:
    keys = jax.random.split(jax.random.key(seed), 11)
    return {
        "rhs": normal_values(keys[0], (ELEMS, FUNCS, BLOCK), 1.0, 6.0, ((0, 128),), jnp.float32),
        "diag_block": draw_diag_block(jax.random.fold_in(keys[10], 71), 0),
        "precond": draw_precond(jax.random.fold_in(keys[10], 71), 0),
        "face_block": normal_values(keys[3], (ELEMS, FACES, BLOCK, BLOCK), (44 * BLOCK) ** -0.5, 0.0546875, ((0, 128),), jnp.float32),
        "face_nbr": draw_face_nbr(jax.random.fold_in(keys[10], 71), 0),
        "pair_recv_elem": plant(jax.random.randint(keys[5], (PAIRS,), 0, E_DEV), jax.random.fold_in(keys[5], 1), 0, E_DEV - 1).astype(jnp.int32),
        "pair_donor_dev": draw_pair_donor_dev(jax.random.fold_in(keys[10], 71), 0),
        "pair_donor_elem": plant(jax.random.randint(keys[7], (PAIRS,), 0, E_DEV), jax.random.fold_in(keys[7], 1), 0, E_DEV - 1).astype(jnp.int32),
        "pair_weight": jnp.clip(jnp.exp(math.log(0.6) - 1.7917595 * jax.random.uniform(keys[8], (PAIRS,), jnp.float32) ** shard_levels(keys[8], (PAIRS,), ((0, 128),), -0.2, 0.2)), 0.1, 0.6),
        "fringe_count": draw_fringe_count(jax.random.fold_in(keys[10], 71), 0),
    }


highest = lax.Precision.HIGHEST


def transposed(blocks, values):
    return jnp.einsum('eab,era->erb', blocks, values, precision=highest)


def donor_slots(donor_devices, sender):
    half = NEAR // 2
    distance = (donor_devices - sender + N_DOM) % N_DOM
    signed = jnp.where(distance <= half, distance, distance - N_DOM)
    bucket = jnp.where(signed < 0, signed + half, signed + half - 1)
    bucket = jnp.where(distance == N_DOM // 2, NEAR - 1, bucket).astype(jnp.int32)
    onehot = (bucket[:, None] == jnp.arange(NEAR, dtype=jnp.int32)[None, :]).astype(jnp.int32)
    position = jnp.sum((jnp.cumsum(onehot, axis=0) - 1) * onehot, axis=1).astype(jnp.int32)
    return (bucket * CAP + position).astype(jnp.int32)


def reference(rhs, diag_block, precond, face_block, face_nbr, pair_recv_elem, pair_donor_dev, pair_donor_elem, pair_weight, fringe_count):
    def off_diagonal(values):
        def face_step(device, accumulated):
            begin = (device * E_DEV).astype(jnp.int32)
            blocks = lax.dynamic_slice_in_dim(face_block, begin, E_DEV, 0)
            portion = lax.dynamic_slice_in_dim(values, begin, E_DEV, 0)
            neighbours = lax.dynamic_slice_in_dim(face_nbr, begin, E_DEV, 0)
            contrib = jnp.einsum('efab,era->efrb', blocks, portion, precision=highest)
            return accumulated.at[neighbours.reshape(-1)].add(contrib.reshape(E_DEV * FACES, FUNCS, BLOCK))

        faces_sum = lax.fori_loop(0, N_DOM, face_step, jnp.zeros((ELEMS, FUNCS, BLOCK), jnp.float32))

        def pair_step(device, accumulated):
            sender = jnp.asarray(device).astype(jnp.int32)
            begin = (sender * R_DEV).astype(jnp.int32)
            receptors = lax.dynamic_slice_in_dim(pair_recv_elem, begin, R_DEV, 0) + (sender * E_DEV).astype(jnp.int32)
            donor_devices = lax.dynamic_slice_in_dim(pair_donor_dev[:, 0], begin, R_DEV, 0)
            slots = donor_slots(donor_devices, sender)
            donors = donor_devices * E_DEV + pair_donor_elem[(donor_devices * R_DEV + slots).astype(jnp.int32)]
            active = jnp.arange(R_DEV, dtype=jnp.int32) < fringe_count[sender]
            weights = jnp.where(active, lax.dynamic_slice_in_dim(pair_weight, begin, R_DEV, 0), jnp.float32(0.0))
            payload = (weights[:, None, None] * values[receptors]).astype(jnp.bfloat16)
            payload = lax.optimization_barrier(payload)
            return accumulated.at[donors].add(payload.astype(jnp.float32))

        fringe_sum = lax.fori_loop(0, N_DOM, pair_step, jnp.zeros((ELEMS, FUNCS, BLOCK), jnp.float32))
        return faces_sum - fringe_sum

    adjoint = jnp.zeros((ELEMS, FUNCS, BLOCK), jnp.float32)
    for subiter in range(SUBITS):
        if subiter == 0:
            residual = rhs
        else:
            residual = rhs - transposed(diag_block, adjoint) - off_diagonal(adjoint)
        update = transposed(precond, residual)
        for repeat in range(SWEEPS - 1):
            update = transposed(precond, residual - off_diagonal(update))
        adjoint = adjoint + update
    return adjoint
```

```python
import jax
import jax.numpy as jnp
from jax import lax
from jax.experimental import pallas as pl
from jax.experimental.pallas import tpu as pltpu
from jax.sharding import PartitionSpec as P

E = 8
R = 16
B = 320
FACES = 6
PAIRS = 16
OFFSETS = (-4, -3, -2, -1, 1, 2, 3, 64)
FAR = (0, 1, 2, 5, 6, 7)
MIB = 1024 * 1024
f32 = jnp.float32
bf16 = jnp.bfloat16

VM = pl.BlockSpec(memory_space=pltpu.VMEM)
SM = pl.BlockSpec(memory_space=pltpu.SMEM)
ANY = pl.BlockSpec(memory_space=pl.ANY)


def dot(a, b):
    return jnp.dot(a, b, preferred_element_type=f32)


def halves(x):
    high = x.astype(bf16)
    return high, (x - high.astype(f32)).astype(bf16)


def product(x, high, low):
    x_high, x_low = halves(x)
    both = dot(jnp.concatenate([x_high, x_low], axis=0), high)
    return both[:R] + both[R:] + dot(x_high, low)


def route_pairs(me, dev, order):
    counts = [jnp.int32(0)] * len(OFFSETS)
    for p in range(PAIRS):
        distance = lax.rem(dev[p] - me + 128, 128)
        bucket = jnp.where(distance <= 4, distance + 3, distance - 124)
        bucket = jnp.where(distance == 64, 7, bucket)
        position = jnp.int32(0)
        for k in range(len(OFFSETS)):
            hit = (bucket == k).astype(jnp.int32)
            position = position + hit * counts[k]
            counts[k] = counts[k] + hit
        order[bucket * 2 + position] = p


def emit_pairs(v, nbr, recv, weight, count, order, outs):
    for slot in range(PAIRS):
        p = order[slot]
        scale = jnp.where(p < count[0], weight[p], f32(0.0))
        outs[slot // 2][slot % 2] = (scale * v[recv[p]]).astype(bf16)


def emit_faces(e, u, face_of, me, nbr, acc):
    ub = u.astype(bf16)
    for f in range(FACES):
        n = nbr[e * FACES + f]
        side = lax.rem(lax.div(n, E) - me + 129, 128)
        target = side * E + lax.rem(n, E)
        acc[target] += dot(ub, face_of(f))


def finish(acc, own, prev, nxt):
    own[...] = acc[E : 2 * E]
    prev[0:E] = acc[0:E].astype(bf16)
    nxt[0:E] = acc[2 * E :].astype(bf16)


def pair_outs(prev, nxt, far):
    far = list(far)
    return far[:3] + [prev.at[E : E + 2], nxt.at[E : E + 2]] + far[3:]


def first_kernel(me, nbr, recv, dev, weight, count, rhs, precond, face,
                 fb, ph, plo, u_out, own, prev, nxt, f0, f1, f2, f3, f4, f5,
                 fbuf, pbuf, acc, order, fsem, psem):
    slots = fbuf.shape[0]

    def fetch_f(e):
        return pltpu.make_async_copy(face.at[e], fbuf.at[e % slots], fsem.at[e % slots])

    def fetch_p(e):
        return pltpu.make_async_copy(precond.at[e], pbuf.at[e], psem.at[e])

    for e in range(E):
        fetch_p(e).start()
        if e < slots:
            fetch_f(e).start()
    route_pairs(me[0], dev, order)
    acc[...] = jnp.zeros_like(acc)
    for e in range(E):
        fetch_p(e).wait()
        high, low = halves(pbuf[e])
        ph[e] = high
        plo[e] = low
        u_out[e] = product(rhs[e], high, low)
    emit_pairs(u_out, nbr, recv, weight, count, order, pair_outs(prev, nxt, (f0, f1, f2, f3, f4, f5)))
    for e in range(E):
        fetch_f(e).wait()
        for f in range(FACES):
            fb[e, f] = fbuf[e % slots, f].astype(bf16)
        if e + slots < E:
            fetch_f(e + slots).start()
        emit_faces(e, u_out[e], lambda f: fb[e, f], me[0], nbr, acc)
    finish(acc, own, prev, nxt)


def combine(own_in, prev_in, nxt_in, far_in, donor, total):
    total[...] = own_in[...] + prev_in[0:E].astype(f32) + nxt_in[0:E].astype(f32)
    sources = list(far_in[:3]) + [nxt_in.at[E : E + 2], prev_in.at[E : E + 2]] + list(far_in[3:])
    for slot in range(PAIRS):
        total[donor[slot]] -= sources[slot // 2][slot % 2].astype(f32)


def step_kernel(with_sum, me, nbr, recv, dev, weight, count, donor, base, *refs):
    if with_sum:
        a_in, *refs = refs
    (fb, ph, plo, own_in, prev_in, nxt_in, i0, i1, i2, i3, i4, i5,
     x_out, v_out, own, prev, nxt, f0, f1, f2, f3, f4, f5, acc, total, order) = refs
    route_pairs(me[0], dev, order)
    acc[...] = jnp.zeros_like(acc)
    combine(own_in, prev_in, nxt_in, (i0, i1, i2, i3, i4, i5), donor, total)
    for e in range(E):
        x = base[e] - total[e]
        x_out[e] = x
        u = product(x, ph[e], plo[e])
        v_out[e] = u + a_in[e] if with_sum else u
    emit_pairs(v_out, nbr, recv, weight, count, order, pair_outs(prev, nxt, (f0, f1, f2, f3, f4, f5)))
    for e in range(E):
        emit_faces(e, v_out[e], lambda f: fb[e, f], me[0], nbr, acc)
    finish(acc, own, prev, nxt)


def last_kernel(donor, base, a_in, ph, plo, own_in, prev_in, nxt_in, i0, i1, i2, i3, i4, i5, out, total):
    combine(own_in, prev_in, nxt_in, (i0, i1, i2, i3, i4, i5), donor, total)
    for e in range(E):
        out[e] = a_in[e] + product(base[e] - total[e], ph[e], plo[e])


def split_kernel(diag, dh, dl):
    for e in range(E):
        dh[e], dl[e] = halves(diag[e])


def diag_kernel(rhs, v, dh, dl, out):
    for e in range(E):
        out[e] = rhs[e] - product(v[e], dh[e], dl[e])


def vm(shape, dtype):
    return pltpu.VMEM(shape, dtype)


VALUE = jax.ShapeDtypeStruct((E, R, B), f32)
SIDE = jax.ShapeDtypeStruct((E + 2, R, B), bf16)
PAIR = jax.ShapeDtypeStruct((2, R, B), bf16)
BLOCK = (E, B, B)


def params(mib):
    return pltpu.CompilerParams(vmem_limit_bytes=mib * MIB)


def pin(x):
    return pltpu.with_memory_space_constraint(x, pltpu.VMEM)


def shifted(value, steps):
    count = lax.axis_size("dom")
    return lax.ppermute(value, "dom", [(s, (s + steps) % count) for s in range(count)])


def exchange(prev, nxt, far):
    got = [shifted(f, OFFSETS[k]) for f, k in zip(far, FAR)]
    return shifted(nxt, 1), shifted(prev, -1), *got


def local(rhs, diag_block, precond, face_block, face_nbr, pair_recv_elem, pair_donor_dev,
          pair_donor_elem, pair_weight, fringe_count):
    me = lax.axis_index("dom").astype(jnp.int32).reshape(1)
    ints = (me, face_nbr.reshape(-1), pair_recv_elem, pair_donor_dev.reshape(-1), pair_weight, fringe_count)

    fb, ph, plo, u, own, prev, nxt, *far = pl.pallas_call(
        first_kernel,
        in_specs=[SM] * 6 + [VM, ANY, ANY],
        out_specs=[VM] * 13,
        out_shape=[vm((E, FACES, B, B), bf16), vm(BLOCK, bf16), vm(BLOCK, bf16), VALUE, VALUE, SIDE, SIDE] + [PAIR] * 6,
        scratch_shapes=[
            pltpu.VMEM((3, FACES, B, B), f32), pltpu.VMEM(BLOCK, f32), pltpu.VMEM((3 * E, R, B), f32),
            pltpu.SMEM((PAIRS,), jnp.int32), pltpu.SemaphoreType.DMA((3,)), pltpu.SemaphoreType.DMA((E,)),
        ],
        compiler_params=params(24),
        name="first",
    )(*ints, rhs, pltpu.with_memory_space_constraint(precond, pltpu.HBM), pltpu.with_memory_space_constraint(face_block, pltpu.HBM))
    fb, ph, plo = pin(fb), pin(ph), pin(plo)
    dh, dl = pl.pallas_call(
        split_kernel,
        in_specs=[VM], out_specs=[VM, VM], out_shape=[vm(BLOCK, bf16), vm(BLOCK, bf16)],
        compiler_params=params(24), name="split",
    )(diag_block)
    dh, dl = pin(dh), pin(dl)

    def step(base, a, own, got):
        args = [base] + ([a] if a is not None else [])
        x, v, own, prev, nxt, *far = pl.pallas_call(
            lambda *refs: step_kernel(a is not None, *refs),
            in_specs=[SM] * 7 + [VM] * (len(args) + 12),
            out_specs=[VM] * 11,
            out_shape=[VALUE, VALUE, VALUE, SIDE, SIDE] + [PAIR] * 6,
            scratch_shapes=[pltpu.VMEM((3 * E, R, B), f32), pltpu.VMEM((E, R, B), f32), pltpu.SMEM((PAIRS,), jnp.int32)],
            compiler_params=params(24),
            name="step",
        )(*ints, pair_donor_elem, *args, fb, ph, plo, own, *got)
        return x, v, own, exchange(prev, nxt, far)

    def diag(v):
        return pl.pallas_call(
            diag_kernel, in_specs=[VM] * 4, out_specs=VM, out_shape=VALUE, compiler_params=params(24), name="diag",
        )(rhs, v, dh, dl)

    got = exchange(prev, nxt, far)
    _, a1, own, got = step(rhs, None, own, got)
    r1, _, own, got = step(diag(a1), None, own, got)
    _, a2, own, got = step(r1, a1, own, got)
    r2, _, own, got = step(diag(a2), None, own, got)
    return pl.pallas_call(
        last_kernel,
        in_specs=[SM] + [VM] * 13, out_specs=VM, out_shape=VALUE,
        scratch_shapes=[pltpu.VMEM((E, R, B), f32)],
        compiler_params=params(24), name="last",
    )(pair_donor_elem, r2, a2, ph, plo, own, *got)


def solution(mesh):
    dom = P("dom")
    return jax.shard_map(local, mesh=mesh, in_specs=(dom,) * 10, out_specs=dom, check_vma=False)
```

```python
import jax
import jax.numpy as jnp
from jax import lax
from jax.experimental import pallas as pl
from jax.experimental.pallas import tpu as pltpu
from jax.sharding import PartitionSpec as P

E = 8
R = 16
B = 320
FACES = 6
PAIRS = 16
N = 128
GROUP = 8
LIST = E * FACES + 2 * GROUP
AHEAD = 3
MIB = 1024 * 1024
f32 = jnp.float32
bf16 = jnp.bfloat16

VM = pl.BlockSpec(memory_space=pltpu.VMEM)
SM = pl.BlockSpec(memory_space=pltpu.SMEM)
ANY = pl.BlockSpec(memory_space=pl.ANY)


def dot(a, b):
    return jnp.dot(a, b, preferred_element_type=f32)


def halves(x):
    high = x.astype(bf16)
    return high, (x - high.astype(f32)).astype(bf16)


def product(x, high, low):
    x_high, x_low = halves(x)
    both = dot(jnp.concatenate([x_high, x_low], axis=0), high)
    return both[:R] + both[R:] + dot(x_high, low)


def pair(k):
    return pl.ds(2 * k, 2)


def fill_tables(me, nbr, recv, dev, weight, count, ahead, faces, targets, bounds, rows, scales):
    core = lax.bitwise_and(me, 1)
    near_side = jnp.where(core == 0, 0, 2)
    for i in range(LIST):
        faces[i] = 0
        targets[i] = 2 * E
    kinds = []
    total = jnp.int32(0)
    for e in range(E):
        for f in range(FACES):
            n = nbr[e, f]
            side = lax.bitwise_and(lax.shift_right_logical(n, 3) - me + 129, 127)
            near = side == near_side
            row = lax.bitwise_and(n, 7)
            ahead[e * FACES + f] = jnp.where(near, row, E)
            kinds.append((near, jnp.where(near | (side == 1), row, row + E)))
            total = total + near.astype(jnp.int32)
    groups = lax.div(total + GROUP - 1, GROUP)
    bounds[0] = groups
    bounds[1] = groups + lax.div(E * FACES - total + GROUP - 1, GROUP)
    first, second = jnp.int32(0), groups * GROUP
    for i, (near, row) in enumerate(kinds):
        at = jnp.where(near, first, second)
        faces[at] = i
        targets[at] = row
        step = near.astype(jnp.int32)
        first, second = first + step, second + 1 - step
    counts = [jnp.int32(0)] * 8
    for p in range(PAIRS):
        distance = lax.bitwise_and(dev[p] - me + 128, 127)
        bucket = jnp.where(distance <= 4, distance + 3, distance - 124)
        bucket = jnp.where(distance == 64, 7, bucket)
        position = jnp.int32(0)
        for k in range(8):
            hit = (bucket == k).astype(jnp.int32)
            position = position + hit * counts[k]
            counts[k] = counts[k] + hit
        rows[bucket * 2 + position] = recv[p]
        scales[bucket * 2 + position] = jnp.where(p < count[0], weight[p], f32(0.0))


def emit_pairs(core, v, rows, scales, pay, early, half):
    for slot in range(PAIRS):
        pay[slot] = (scales[slot] * v[rows[slot]]).astype(bf16)
    half[...] = pay[14:16]
    for j, (k0, k1) in enumerate(((5, 1), (6, 2), (0, 6), (1, 6))):
        early[2 * j : 2 * j + 2] = pay[pair(jnp.where(core == 0, k0, k1))]


def add_faces(low, high, v, fb, faces, targets, acc):
    acc[...] = jnp.zeros_like(acc)

    def group(g, carry):
        terms = []
        for j in range(GROUP):
            face = faces[g * GROUP + j]
            terms.append(dot(v[lax.div(face, FACES)], fb[face]))
        for j in range(GROUP):
            acc[targets[g * GROUP + j]] += terms[j]
        return carry

    lax.fori_loop(low, high, group, 0)


def finish_near(core, acc, pay, near):
    near[0:E] = acc[0:E].astype(bf16)
    near[8:10] = pay[pair(jnp.where(core == 0, 3, 4))]
    near[12:14] = pay[pair(jnp.where(core == 0, 2, 5))]


def start_kernel(me, nbr, recv, dev, weight, count, rhs, precond, face,
                 ahead, faces, targets, bounds, rows, scales, ph, plo, fb, v_out, pay, early, half,
                 pbuf, fbuf, v, psem, fsem):
    def fetch(e):
        return pltpu.make_async_copy(precond.at[e], pbuf.at[e], psem.at[e])

    def fetch_face(e):
        return pltpu.make_async_copy(face.at[e], fbuf.at[e], fsem.at[e])

    for e in range(E):
        fetch(e).start()
    for e in range(AHEAD):
        fetch_face(e).start()
    fill_tables(me[0], nbr, recv, dev, weight, count, ahead, faces, targets, bounds, rows, scales)
    for e in range(E):
        fetch(e).wait()
        high, low = halves(pbuf[e])
        ph[e] = high
        plo[e] = low
        v[e] = product(rhs[e], high, low)
        v_out[e] = v[e].astype(bf16)
    emit_pairs(lax.bitwise_and(me[0], 1), v, rows, scales, pay, early, half)
    for e in range(AHEAD):
        fetch_face(e).wait()
        for f in range(FACES):
            fb[e * FACES + f] = fbuf[e, f].astype(bf16)


def load_kernel(me, ahead, v, pay, fb_in, face, fb, near, fbuf, acc, fsem):
    def fetch(e):
        return pltpu.make_async_copy(face.at[e], fbuf.at[e - AHEAD], fsem.at[e - AHEAD])

    for e in range(AHEAD, E):
        fetch(e).start()
    acc[...] = jnp.zeros_like(acc)
    for e in range(E):
        if e >= AHEAD:
            fetch(e).wait()
            for f in range(FACES):
                fb[e * FACES + f] = fbuf[e - AHEAD, f].astype(bf16)
        terms = [dot(v[e], fb[e * FACES + f]) for f in range(FACES)]
        for f in range(FACES):
            acc[ahead[e * FACES + f]] += terms[f]
    finish_near(lax.bitwise_and(me[0], 1), acc, pay, near)


def near_kernel(me, faces, targets, bounds, v, pay, fb, near, acc):
    add_faces(0, bounds[0], v, fb, faces, targets, acc)
    finish_near(lax.bitwise_and(me[0], 1), acc, pay, near)


def rest_kernel(me, faces, targets, bounds, v, pay, fb, own, late, acc):
    core = lax.bitwise_and(me[0], 1)
    add_faces(bounds[0], bounds[1], v, fb, faces, targets, acc)
    own[...] = acc[0:E]
    late[8:16] = acc[E : 2 * E].astype(bf16)
    late[16:18] = pay[pair(jnp.where(core == 0, 4, 3))]


def bundle_kernel(me, got, pay, near_in, near, skip):
    core = lax.bitwise_and(me[0], 1)
    near[10:12] = got[pair(jnp.where(core == 0, 1, 0))]
    near[14:16] = got[pair(jnp.where(core == 0, 0, 1))]
    skip[0:2] = jnp.where(core == 0, got[4:6], pay[0:2])
    skip[2:4] = got[6:8]
    skip[4:6] = got[4:6]


def take(total, donor, k, row, live=None):
    for c in range(2):
        target = donor[2 * k + c]
        if live is not None:
            target = jnp.where(live, target, E)
        total[target] -= row[c].astype(f32)


def gather_kernel(me, donor, own, near, skip, half, late_in, out, late, total):
    core = lax.bitwise_and(me[0], 1)
    late[0:4] = near[12:16]
    late[4:8] = skip[0:4]
    total[0:E] = own[...] + near[0:E].astype(f32)
    total[E] = jnp.zeros((R, B), f32)
    take(total, donor, jnp.where(core == 0, 4, 3), near[8:10])
    take(total, donor, jnp.where(core == 0, 5, 2), near[10:12])
    take(total, donor, 7, half[...])
    take(total, donor, 0, skip[4:6], core == 0)
    out[...] = total[0:E]


def settle(core, donor, total_in, late, total):
    total[0:E] = total_in[...] + late[8:16].astype(f32)
    total[E] = jnp.zeros((R, B), f32)
    take(total, donor, jnp.where(core == 0, 2, 5), late[0:2])
    take(total, donor, jnp.where(core == 0, 1, 6), late[2:4])
    take(total, donor, jnp.where(core == 0, 6, 0), late[4:6])
    take(total, donor, 1, late[6:8], core == 1)
    take(total, donor, jnp.where(core == 0, 3, 4), late[16:18])


def update_kernel(with_sum, keep_x, me, donor, rows, scales, base, *refs):
    if with_sum:
        a_in, *refs = refs
    total_in, late, ph, plo, out, v_out, pay, early, half, total, v = refs
    core = lax.bitwise_and(me[0], 1)
    settle(core, donor, total_in, late, total)
    for e in range(E):
        x = base[e] - total[e]
        u = product(x, ph[e], plo[e])
        if with_sum:
            u = u + a_in[e]
        v[e] = u
        v_out[e] = u.astype(bf16)
        out[e] = x if keep_x else u
    emit_pairs(core, v, rows, scales, pay, early, half)


def last_kernel(me, donor, base, a_in, total_in, late, ph, plo, out, total):
    settle(lax.bitwise_and(me[0], 1), donor, total_in, late, total)
    for e in range(E):
        out[e] = a_in[e] + product(base[e] - total[e], ph[e], plo[e])


def split_kernel(diag, dh, dl):
    for e in range(E):
        dh[e], dl[e] = halves(diag[e])


def diag_kernel(rhs, v, dh, dl, out):
    for e in range(E):
        out[e] = rhs[e] - product(v[e], dh[e], dl[e])


VALUE = jax.ShapeDtypeStruct((E, R, B), f32)
BLOCK = (E, B, B)


def rows_of(count):
    return pltpu.VMEM((count, R, B), bf16)


def call(kernel, name, ins, outs, scratch=(), **options):
    return pl.pallas_call(
        kernel,
        in_specs=ins,
        out_specs=[SM if o.memory_space == pltpu.SMEM else VM for o in outs],
        out_shape=outs,
        scratch_shapes=scratch,
        compiler_params=pltpu.CompilerParams(vmem_limit_bytes=20 * MIB),
        name=name,
        **options,
    )


def pin(x, space=pltpu.VMEM):
    return pltpu.with_memory_space_constraint(x, space)


def swap(x):
    return lax.ppermute(x, "dom", [(s, s ^ 1) for s in range(N)])


def near_swap(x):
    return lax.ppermute(x, "dom", [(s, (s + (1 if s % 2 else -1)) % N) for s in range(N)])


def skip_shift(x):
    return lax.ppermute(x, "dom", [(s, (s + (-5 if s % 2 else 5)) % N) for s in range(N)])


def half_swap(x):
    return lax.ppermute(x, "dom", [(s, s ^ 64) for s in range(N)])


def local(rhs, diag_block, precond, face_block, face_nbr, pair_recv_elem, pair_donor_dev,
          pair_donor_elem, pair_weight, fringe_count):
    me = lax.axis_index("dom").astype(jnp.int32).reshape(1)
    donor = pair_donor_elem
    value = pltpu.VMEM((E, R, B), f32)
    total = pltpu.VMEM((E + 1, R, B), f32)
    acc = pltpu.VMEM((2 * E + 1, R, B), f32)
    sent = [rows_of(E), rows_of(PAIRS), rows_of(8), rows_of(2)]
    hbm = lambda x: pin(x, pltpu.HBM)
    smem = lambda x: pin(x, pltpu.SMEM)
    table = lambda n, dtype=jnp.int32: pltpu.SMEM((n,), dtype)

    ahead, faces, targets, bounds, rows, scales, ph, plo, fb, v, pay, early, half = call(
        start_kernel, "start", [SM] * 6 + [VM, ANY, ANY],
        [table(E * FACES), table(LIST), table(LIST), table(2), table(PAIRS), table(PAIRS, f32),
         pltpu.VMEM(BLOCK, bf16), pltpu.VMEM(BLOCK, bf16), pltpu.VMEM((E * FACES, B, B), bf16)] + sent,
        [pltpu.VMEM(BLOCK, f32), pltpu.VMEM((AHEAD, FACES, B, B), f32), value,
         pltpu.SemaphoreType.DMA((E,)), pltpu.SemaphoreType.DMA((AHEAD,))],
    )(me, hbm(face_nbr), hbm(pair_recv_elem), hbm(pair_donor_dev.reshape(-1)), hbm(pair_weight), fringe_count,
      hbm(rhs), hbm(precond), hbm(face_block))
    ahead, faces, targets, bounds = smem(ahead), smem(faces), smem(targets), smem(bounds)
    rows, scales, ph, plo = smem(rows), smem(scales), pin(ph), pin(plo)

    got = swap(early)
    fb, near = call(
        load_kernel, "load", [SM, SM, VM, VM, VM, ANY],
        [pltpu.VMEM((E * FACES, B, B), bf16), rows_of(16)],
        [pltpu.VMEM((E - AHEAD, FACES, B, B), f32), acc, pltpu.SemaphoreType.DMA((E - AHEAD,))],
        input_output_aliases={4: 0},
    )(me, ahead, pin(v), pin(pay), pin(fb), hbm(face_block))
    fb = pin(fb)

    dh, dl = call(split_kernel, "split", [VM], [pltpu.VMEM(BLOCK, bf16)] * 2)(diag_block)
    dh, dl = pin(dh), pin(dl)

    def exchange(v, near, half, pay, got):
        near, skip = call(
            bundle_kernel, "bundle", [SM, VM, VM, VM], [rows_of(16), rows_of(6)], input_output_aliases={3: 0},
        )(me, pin(got), pin(pay), pin(near))
        near, skip, half = near_swap(near), skip_shift(skip), half_swap(half)
        own, late = call(
            rest_kernel, "rest", [SM] * 4 + [VM] * 3, [value, rows_of(18)], [acc],
        )(me, faces, targets, bounds, pin(v), pin(pay), fb)
        sums, late = call(
            gather_kernel, "gather", [SM, SM] + [VM] * 5, [value, rows_of(18)], [total], input_output_aliases={6: 1},
        )(me, donor, pin(own), pin(near), pin(skip), pin(half), pin(late))
        return sums, swap(late)

    def step(base, a, keep_x, sums, late):
        args = [pin(base)] + ([pin(a)] if a is not None else [])
        out, v, pay, early, half = call(
            lambda *refs: update_kernel(a is not None, keep_x, *refs), "update", [SM] * 4 + [VM] * (len(args) + 4),
            [value] + sent, [total, value],
        )(me, donor, rows, scales, *args, pin(sums), pin(late), ph, plo)
        got = swap(early)
        near = call(
            near_kernel, "near", [SM] * 4 + [VM] * 3, [rows_of(16)], [acc],
        )(me, faces, targets, bounds, pin(v), pin(pay), fb)[0]
        return out, exchange(v, near, half, pay, got)

    def diag(v):
        return call(diag_kernel, "diag", [VM] * 4, [value])(rhs, pin(v), dh, dl)[0]

    sums = exchange(v, near, half, pay, got)
    a1, sums = step(rhs, None, False, *sums)
    r1, sums = step(diag(a1), None, True, *sums)
    a2, sums = step(r1, a1, False, *sums)
    r2, sums = step(diag(a2), None, True, *sums)
    return pl.pallas_call(
        last_kernel, in_specs=[SM, SM] + [VM] * 6, out_specs=VM, out_shape=VALUE, scratch_shapes=[total],
        compiler_params=pltpu.CompilerParams(vmem_limit_bytes=20 * MIB), name="last",
    )(me, donor, pin(r2), pin(a2), *map(pin, sums), ph, plo)


def solution(mesh):
    dom = P("dom")
    return jax.shard_map(local, mesh=mesh, in_specs=(dom,) * 10, out_specs=dom, check_vma=False)
```

```python
import jax
import jax.numpy as jnp
from jax import lax
from jax.experimental import pallas as pl
from jax.experimental.pallas import tpu as pltpu
from jax.sharding import PartitionSpec as P

E = 8
R = 16
B = 320
FACES = 6
PAIRS = 16
N = 128
GROUP = 8
LIST = E * FACES + 2 * GROUP
AHEAD = 2
MIB = 1024 * 1024
f32 = jnp.float32
bf16 = jnp.bfloat16

VM = pl.BlockSpec(memory_space=pltpu.VMEM)
SM = pl.BlockSpec(memory_space=pltpu.SMEM)
ANY = pl.BlockSpec(memory_space=pl.ANY)


def dot(a, b):
    return jnp.dot(a, b, preferred_element_type=f32)


def halves(x):
    high = x.astype(bf16)
    return high, (x - high.astype(f32)).astype(bf16)


def product(x, high, low):
    x_high, x_low = halves(x)
    both = dot(jnp.concatenate([x_high, x_low], axis=0), high)
    return both[:R] + both[R:] + dot(x_high, low)


def pair(k):
    return pl.ds(2 * k, 2)


def fill_tables(me, nbr, recv, dev, weight, count, ahead, faces, targets, bounds, rows, scales):
    core = lax.bitwise_and(me, 1)
    near_side = jnp.where(core == 0, 0, 2)
    for i in range(LIST):
        faces[i] = 0
        targets[i] = 2 * E
    kinds = []
    total = jnp.int32(0)
    for e in range(E):
        for f in range(FACES):
            n = nbr[e, f]
            side = lax.bitwise_and(lax.shift_right_logical(n, 3) - me + 129, 127)
            near = side == near_side
            row = lax.bitwise_and(n, 7)
            ahead[e * FACES + f] = jnp.where(near, row, E)
            kinds.append((near, jnp.where(near | (side == 1), row, row + E)))
            total = total + near.astype(jnp.int32)
    groups = lax.div(total + GROUP - 1, GROUP)
    bounds[0] = groups
    bounds[1] = groups + lax.div(E * FACES - total + GROUP - 1, GROUP)
    first, second = jnp.int32(0), groups * GROUP
    for i, (near, row) in enumerate(kinds):
        at = jnp.where(near, first, second)
        faces[at] = i
        targets[at] = row
        step = near.astype(jnp.int32)
        first, second = first + step, second + 1 - step
    counts = [jnp.int32(0)] * 8
    for p in range(PAIRS):
        distance = lax.bitwise_and(dev[p] - me + 128, 127)
        bucket = jnp.where(distance <= 4, distance + 3, distance - 124)
        bucket = jnp.where(distance == 64, 7, bucket)
        position = jnp.int32(0)
        for k in range(8):
            hit = (bucket == k).astype(jnp.int32)
            position = position + hit * counts[k]
            counts[k] = counts[k] + hit
        rows[bucket * 2 + position] = recv[p]
        scales[bucket * 2 + position] = jnp.where(p < count[0], weight[p], f32(0.0))


def emit_pairs(core, v, rows, scales, pay, early, half):
    for slot in range(PAIRS):
        pay[slot] = (scales[slot] * v[rows[slot]]).astype(bf16)
    half[...] = pay[14:16]
    for j, (k0, k1) in enumerate(((5, 1), (6, 2), (0, 6), (1, 6))):
        early[2 * j : 2 * j + 2] = pay[pair(jnp.where(core == 0, k0, k1))]


def add_faces(low, high, v, fb, faces, targets, acc):
    acc[...] = jnp.zeros_like(acc)

    def group(g, carry):
        terms = []
        for j in range(GROUP):
            face = faces[g * GROUP + j]
            terms.append(dot(v[lax.div(face, FACES)], fb[face]))
        for j in range(GROUP):
            acc[targets[g * GROUP + j]] += terms[j]
        return carry

    lax.fori_loop(low, high, group, 0)


def finish_near(core, acc, pay, near):
    near[0:E] = acc[0:E].astype(bf16)
    near[8:10] = pay[pair(jnp.where(core == 0, 3, 4))]
    near[12:14] = pay[pair(jnp.where(core == 0, 2, 5))]


def start_kernel(me, nbr, recv, dev, weight, count, rhs, precond, face,
                 ahead, faces, targets, bounds, rows, scales, ph, plo, fb, v_out, pay, early, half,
                 pbuf, fbuf, v, psem, fsem):
    def fetch(e):
        return pltpu.make_async_copy(precond.at[e], pbuf.at[e], psem.at[e])

    def fetch_face(e):
        return pltpu.make_async_copy(face.at[e], fbuf.at[e], fsem.at[e])

    for e in range(E):
        fetch(e).start()
    for e in range(AHEAD):
        fetch_face(e).start()
    fill_tables(me[0], nbr, recv, dev, weight, count, ahead, faces, targets, bounds, rows, scales)
    for e in range(E):
        fetch(e).wait()
        high, low = halves(pbuf[e])
        ph[e] = high
        plo[e] = low
        v[e] = product(rhs[e], high, low)
        v_out[e] = v[e].astype(bf16)
    emit_pairs(lax.bitwise_and(me[0], 1), v, rows, scales, pay, early, half)
    for e in range(AHEAD):
        fetch_face(e).wait()
        for f in range(FACES):
            fb[e * FACES + f] = fbuf[e, f].astype(bf16)


def load_kernel(me, ahead, v, pay, fb_in, face, fb, near, fbuf, acc, fsem):
    def fetch(e):
        return pltpu.make_async_copy(face.at[e], fbuf.at[e - AHEAD], fsem.at[e - AHEAD])

    for e in range(AHEAD, E):
        fetch(e).start()
    acc[...] = jnp.zeros_like(acc)
    for e in range(E):
        if e >= AHEAD:
            fetch(e).wait()
            for f in range(FACES):
                fb[e * FACES + f] = fbuf[e - AHEAD, f].astype(bf16)
        terms = [dot(v[e], fb[e * FACES + f]) for f in range(FACES)]
        for f in range(FACES):
            acc[ahead[e * FACES + f]] += terms[f]
    finish_near(lax.bitwise_and(me[0], 1), acc, pay, near)


def near_kernel(me, faces, targets, bounds, v, pay, fb, near, acc):
    add_faces(0, bounds[0], v, fb, faces, targets, acc)
    finish_near(lax.bitwise_and(me[0], 1), acc, pay, near)


def rest_split_kernel(me, faces, targets, bounds, v, pay, fb, diag, own, late, dh, dl, acc):
    rest_kernel(me, faces, targets, bounds, v, pay, fb, own, late, acc)
    for e in range(E):
        dh[e], dl[e] = halves(diag[e])


def rest_base_kernel(me, faces, targets, bounds, v, pay, fb, rhs, a, dh, dl, own, late, base, acc):
    rest_kernel(me, faces, targets, bounds, v, pay, fb, own, late, acc)
    for e in range(E):
        base[e] = rhs[e] - product(a[e], dh[e], dl[e])


def rest_kernel(me, faces, targets, bounds, v, pay, fb, own, late, acc):
    core = lax.bitwise_and(me[0], 1)
    add_faces(bounds[0], bounds[1], v, fb, faces, targets, acc)
    own[...] = acc[0:E]
    late[8:16] = acc[E : 2 * E].astype(bf16)
    late[16:18] = pay[pair(jnp.where(core == 0, 4, 3))]


def bundle_kernel(me, got, pay, near_in, near, skip):
    core = lax.bitwise_and(me[0], 1)
    near[10:12] = got[pair(jnp.where(core == 0, 1, 0))]
    near[14:16] = got[pair(jnp.where(core == 0, 0, 1))]
    skip[0:2] = jnp.where(core == 0, got[4:6], pay[0:2])
    skip[2:4] = got[6:8]
    skip[4:6] = got[4:6]


def take(total, donor, k, row, live=None):
    for c in range(2):
        target = donor[2 * k + c]
        if live is not None:
            target = jnp.where(live, target, E)
        total[target] -= row[c].astype(f32)


def relay_kernel(near, skip, after, late_in, late):
    late[0:4] = near[12:16]
    late[4:8] = skip[0:4]


def gather_kernel(me, donor, own, near, skip, half, out, total):
    core = lax.bitwise_and(me[0], 1)
    total[0:E] = own[...] + near[0:E].astype(f32)
    total[E] = jnp.zeros((R, B), f32)
    take(total, donor, jnp.where(core == 0, 4, 3), near[8:10])
    take(total, donor, jnp.where(core == 0, 5, 2), near[10:12])
    take(total, donor, 7, half[...])
    take(total, donor, 0, skip[4:6], core == 0)
    out[...] = total[0:E]


def settle(core, donor, total_in, late, total):
    total[0:E] = total_in[...] + late[8:16].astype(f32)
    total[E] = jnp.zeros((R, B), f32)
    take(total, donor, jnp.where(core == 0, 2, 5), late[0:2])
    take(total, donor, jnp.where(core == 0, 1, 6), late[2:4])
    take(total, donor, jnp.where(core == 0, 6, 0), late[4:6])
    take(total, donor, 1, late[6:8], core == 1)
    take(total, donor, jnp.where(core == 0, 3, 4), late[16:18])


def update_kernel(with_sum, keep_x, me, donor, rows, scales, base, *refs):
    if with_sum:
        a_in, *refs = refs
    total_in, late, ph, plo, out, v_out, pay, early, half, total, v = refs
    core = lax.bitwise_and(me[0], 1)
    settle(core, donor, total_in, late, total)
    for e in range(E):
        x = base[e] - total[e]
        u = product(x, ph[e], plo[e])
        if with_sum:
            u = u + a_in[e]
        v[e] = u
        v_out[e] = u.astype(bf16)
        out[e] = x if keep_x else u
    emit_pairs(core, v, rows, scales, pay, early, half)


def last_kernel(me, donor, base, a_in, total_in, late, ph, plo, out, total):
    settle(lax.bitwise_and(me[0], 1), donor, total_in, late, total)
    for e in range(E):
        out[e] = a_in[e] + product(base[e] - total[e], ph[e], plo[e])


VALUE = jax.ShapeDtypeStruct((E, R, B), f32)
BLOCK = (E, B, B)


def rows_of(count):
    return pltpu.VMEM((count, R, B), bf16)


def call(kernel, name, ins, outs, scratch=(), **options):
    return pl.pallas_call(
        kernel,
        in_specs=ins,
        out_specs=[SM if o.memory_space == pltpu.SMEM else VM for o in outs],
        out_shape=outs,
        scratch_shapes=scratch,
        compiler_params=pltpu.CompilerParams(vmem_limit_bytes=20 * MIB),
        name=name,
        **options,
    )


def pin(x, space=pltpu.VMEM):
    return pltpu.with_memory_space_constraint(x, space)


def swap(x):
    return lax.ppermute(x, "dom", [(s, s ^ 1) for s in range(N)])


def near_swap(x):
    return lax.ppermute(x, "dom", [(s, (s + (1 if s % 2 else -1)) % N) for s in range(N)])


def skip_shift(x):
    return lax.ppermute(x, "dom", [(s, (s + (-5 if s % 2 else 5)) % N) for s in range(N)])


def half_swap(x):
    return lax.ppermute(x, "dom", [(s, s ^ 64) for s in range(N)])


def local(rhs, diag_block, precond, face_block, face_nbr, pair_recv_elem, pair_donor_dev,
          pair_donor_elem, pair_weight, fringe_count):
    me = lax.axis_index("dom").astype(jnp.int32).reshape(1)
    donor = pair_donor_elem
    value = pltpu.VMEM((E, R, B), f32)
    total = pltpu.VMEM((E + 1, R, B), f32)
    acc = pltpu.VMEM((2 * E + 1, R, B), f32)
    sent = [rows_of(E), rows_of(PAIRS), rows_of(8), rows_of(2)]
    hbm = lambda x: pin(x, pltpu.HBM)
    smem = lambda x: pin(x, pltpu.SMEM)
    table = lambda n, dtype=jnp.int32: pltpu.SMEM((n,), dtype)

    ahead, faces, targets, bounds, rows, scales, ph, plo, fb, v, pay, early, half = call(
        start_kernel, "start", [SM] * 6 + [VM, ANY, ANY],
        [table(E * FACES), table(LIST), table(LIST), table(2), table(PAIRS), table(PAIRS, f32),
         pltpu.VMEM(BLOCK, bf16), pltpu.VMEM(BLOCK, bf16), pltpu.VMEM((E * FACES, B, B), bf16)] + sent,
        [pltpu.VMEM(BLOCK, f32), pltpu.VMEM((AHEAD, FACES, B, B), f32), value,
         pltpu.SemaphoreType.DMA((E,)), pltpu.SemaphoreType.DMA((AHEAD,))],
    )(me, hbm(face_nbr), hbm(pair_recv_elem), hbm(pair_donor_dev.reshape(-1)), hbm(pair_weight), fringe_count,
      hbm(rhs), hbm(precond), hbm(face_block))
    ahead, faces, targets, bounds = smem(ahead), smem(faces), smem(targets), smem(bounds)
    rows, scales, ph, plo = smem(rows), smem(scales), pin(ph), pin(plo)

    got = swap(early)
    fb, near = call(
        load_kernel, "load", [SM, SM, VM, VM, VM, ANY],
        [pltpu.VMEM((E * FACES, B, B), bf16), rows_of(16)],
        [pltpu.VMEM((E - AHEAD, FACES, B, B), f32), acc, pltpu.SemaphoreType.DMA((E - AHEAD,))],
        input_output_aliases={4: 0},
    )(me, ahead, pin(v), pin(pay), pin(fb), hbm(face_block))
    fb = pin(fb)

    def exchange(v, near, half, pay, got, kernel=rest_kernel, more=(), outs=()):
        near, skip = call(
            bundle_kernel, "bundle", [SM, VM, VM, VM], [rows_of(16), rows_of(6)], input_output_aliases={3: 0},
        )(me, pin(got), pin(pay), pin(near))
        near, skip, half = near_swap(near), skip_shift(skip), half_swap(half)
        own, late, *others = call(
            kernel, "rest", [SM] * 4 + [VM] * (3 + len(more)), [value, rows_of(18), *outs], [acc],
        )(me, faces, targets, bounds, pin(v), pin(pay), fb, *map(pin, more))
        late = call(
            relay_kernel, "relay", [VM, VM, ANY, VM], [rows_of(18)], input_output_aliases={3: 0},
        )(pin(near), pin(skip), pin(half), pin(late))[0]
        sums = call(
            gather_kernel, "gather", [SM, SM] + [VM] * 4, [value], [total],
        )(me, donor, pin(own), pin(near), pin(skip), pin(half))[0]
        return (sums, swap(late)), *others

    def step(base, a, keep_x, sums, late, with_base=False):
        args = [pin(base)] + ([pin(a)] if a is not None else [])
        out, v, pay, early, half = call(
            lambda *refs: update_kernel(a is not None, keep_x, *refs), "update", [SM] * 4 + [VM] * (len(args) + 4),
            [value] + sent, [total, value],
        )(me, donor, rows, scales, *args, pin(sums), pin(late), ph, plo)
        got = swap(early)
        near = call(
            near_kernel, "near", [SM] * 4 + [VM] * 3, [rows_of(16)], [acc],
        )(me, faces, targets, bounds, pin(v), pin(pay), fb)[0]
        if with_base:
            return out, *exchange(v, near, half, pay, got, rest_base_kernel, (rhs, out, dh, dl), [value])
        return out, *exchange(v, near, half, pay, got)

    sums, dh, dl = exchange(
        v, near, half, pay, got, rest_split_kernel, (diag_block,), [pltpu.VMEM(BLOCK, bf16)] * 2)
    a1, sums, base = step(rhs, None, False, *sums, with_base=True)
    r1, sums = step(base, None, True, *sums)
    a2, sums, base = step(r1, a1, False, *sums, with_base=True)
    r2, sums = step(base, None, True, *sums)
    return pl.pallas_call(
        last_kernel, in_specs=[SM, SM] + [VM] * 6, out_specs=VM, out_shape=VALUE, scratch_shapes=[total],
        compiler_params=pltpu.CompilerParams(vmem_limit_bytes=20 * MIB), name="last",
    )(me, donor, pin(r2), pin(a2), *map(pin, sums), ph, plo)


def solution(mesh):
    dom = P("dom")
    return jax.shard_map(local, mesh=mesh, in_specs=(dom,) * 10, out_specs=dom, check_vma=False)
```

```python
import jax
import jax.numpy as jnp
from jax import lax
from jax.experimental import pallas as pl
from jax.experimental.pallas import tpu as pltpu
from jax.sharding import PartitionSpec as P

E = 8
R = 16
B = 320
FACES = 6
PAIRS = 16
N = 128
GROUP = 8
LIST = E * FACES + 2 * GROUP
AHEAD = 1
DEPTH = 3
MIB = 1024 * 1024
f32 = jnp.float32
bf16 = jnp.bfloat16

VM = pl.BlockSpec(memory_space=pltpu.VMEM)
SM = pl.BlockSpec(memory_space=pltpu.SMEM)
ANY = pl.BlockSpec(memory_space=pl.ANY)


def dot(a, b):
    return jnp.dot(a, b, preferred_element_type=f32)


def halves(x):
    high = x.astype(bf16)
    return high, (x - high.astype(f32)).astype(bf16)


def product(x, high, low):
    x_high, x_low = halves(x)
    both = dot(jnp.concatenate([x_high, x_low], axis=0), high)
    return both[:R] + both[R:] + dot(x_high, low)


def pair(k):
    return pl.ds(2 * k, 2)


def fill_tables(me, nbr, recv, dev, weight, count, faces, targets, bounds, rows, scales):
    core = lax.bitwise_and(me, 1)
    near_side = jnp.where(core == 0, 0, 2)
    for i in range(LIST):
        faces[i] = 0
        targets[i] = 2 * E
    kinds = []
    total = jnp.int32(0)
    for e in range(E):
        for f in range(FACES):
            n = nbr[e, f]
            side = lax.bitwise_and(lax.shift_right_logical(n, 3) - me + 129, 127)
            near = side == near_side
            row = lax.bitwise_and(n, 7)
            kinds.append((near, jnp.where(near | (side == 1), row, row + E)))
            total = total + near.astype(jnp.int32)
    groups = lax.div(total + GROUP - 1, GROUP)
    bounds[0] = groups
    bounds[1] = groups + lax.div(E * FACES - total + GROUP - 1, GROUP)
    first, second = jnp.int32(0), groups * GROUP
    for i, (near, row) in enumerate(kinds):
        at = jnp.where(near, first, second)
        faces[at] = i
        targets[at] = row
        step = near.astype(jnp.int32)
        first, second = first + step, second + 1 - step
    counts = [jnp.int32(0)] * 8
    for p in range(PAIRS):
        distance = lax.bitwise_and(dev[p] - me + 128, 127)
        bucket = jnp.where(distance <= 4, distance + 3, distance - 124)
        bucket = jnp.where(distance == 64, 7, bucket)
        position = jnp.int32(0)
        for k in range(8):
            hit = (bucket == k).astype(jnp.int32)
            position = position + hit * counts[k]
            counts[k] = counts[k] + hit
        rows[bucket * 2 + position] = recv[p]
        scales[bucket * 2 + position] = jnp.where(p < count[0], weight[p], f32(0.0))


def emit_pairs(core, v, rows, scales, pay, early, half):
    for slot in range(PAIRS):
        pay[slot] = (scales[slot] * v[rows[slot]]).astype(bf16)
    half[...] = pay[14:16]
    for j, (k0, k1) in enumerate(((5, 1), (6, 2), (0, 6), (1, 6))):
        early[2 * j : 2 * j + 2] = pay[pair(jnp.where(core == 0, k0, k1))]


def add_faces(low, high, v, fb, faces, targets, acc):
    acc[...] = jnp.zeros_like(acc)

    def group(g, carry):
        terms = []
        for j in range(GROUP):
            face = faces[g * GROUP + j]
            terms.append(dot(v[lax.div(face, FACES)], fb[face]))
        for j in range(GROUP):
            acc[targets[g * GROUP + j]] += terms[j]
        return carry

    lax.fori_loop(low, high, group, 0)


def finish_near(core, acc, pay, near):
    near[0:E] = acc[0:E].astype(bf16)
    near[8:10] = pay[pair(jnp.where(core == 0, 3, 4))]
    near[12:14] = pay[pair(jnp.where(core == 0, 2, 5))]


def start_kernel(me, nbr, recv, dev, weight, count, rhs, precond, face,
                 faces, targets, bounds, rows, scales, ph, plo, fb, v_out, pay, early, half,
                 pbuf, fbuf, v, psem, fsem):
    def fetch(e):
        return pltpu.make_async_copy(precond.at[e], pbuf.at[e], psem.at[e])

    def fetch_face(e):
        return pltpu.make_async_copy(face.at[e], fbuf.at[e], fsem.at[e])

    for e in range(E):
        fetch(e).start()
    for e in range(AHEAD):
        fetch_face(e).start()
    fill_tables(me[0], nbr, recv, dev, weight, count, faces, targets, bounds, rows, scales)
    for e in range(E):
        fetch(e).wait()
        high, low = halves(pbuf[e])
        ph[e] = high
        plo[e] = low
        v[e] = product(rhs[e], high, low)
        v_out[e] = v[e].astype(bf16)
    emit_pairs(lax.bitwise_and(me[0], 1), v, rows, scales, pay, early, half)
    for e in range(AHEAD):
        fetch_face(e).wait()
        for f in range(FACES):
            fb[e * FACES + f] = fbuf[e, f].astype(bf16)


def add_streamed(low, high, v, face, fb, faces, targets, acc, fbuf, sems):
    acc[...] = jnp.zeros_like(acc)

    def each(g, act):
        slot = lax.rem(g - low, DEPTH)
        for j in range(GROUP):
            i = g * GROUP + j
            block = faces[i]

            @pl.when((targets[i] < 2 * E) & (block >= AHEAD * FACES))
            def _():
                source = face.at[lax.div(block, FACES), lax.rem(block, FACES)]
                act(block, fbuf.at[slot, j], pltpu.make_async_copy(source, fbuf.at[slot, j], sems.at[slot, j]))

    def start(block, held, copy):
        copy.start()

    def settle(block, held, copy):
        copy.wait()
        fb[block] = held[...].astype(bf16)

    for ahead in range(DEPTH):
        @pl.when(low + ahead < high)
        def _():
            each(low + ahead, start)

    def group(g, carry):
        each(g, settle)

        @pl.when(g + DEPTH < high)
        def _():
            each(g + DEPTH, start)

        terms = []
        for j in range(GROUP):
            block = faces[g * GROUP + j]
            terms.append(dot(v[lax.div(block, FACES)], fb[block]))
        for j in range(GROUP):
            acc[targets[g * GROUP + j]] += terms[j]
        return carry

    lax.fori_loop(low, high, group, 0)


def load_kernel(me, faces, targets, bounds, v, pay, fb_in, face, near, fb, acc, fbuf, sems):
    add_streamed(0, bounds[0], v, face, fb, faces, targets, acc, fbuf, sems)
    finish_near(lax.bitwise_and(me[0], 1), acc, pay, near)


def near_kernel(me, faces, targets, bounds, v, pay, fb, near, acc):
    add_faces(0, bounds[0], v, fb, faces, targets, acc)
    finish_near(lax.bitwise_and(me[0], 1), acc, pay, near)


def rest_load_kernel(me, faces, targets, bounds, v, pay, fb_in, face, own, late, fb, acc, fbuf, sems):
    add_streamed(bounds[0], bounds[1], v, face, fb, faces, targets, acc, fbuf, sems)
    finish_rest(lax.bitwise_and(me[0], 1), acc, pay, own, late)


def rest_split_kernel(me, faces, targets, bounds, v, pay, fb, rhs, a, diag, own, late, base, dh, dl, acc):
    rest_kernel(me, faces, targets, bounds, v, pay, fb, own, late, acc)
    for e in range(E):
        dh[e], dl[e] = halves(diag[e])
        base[e] = rhs[e] - product(a[e], dh[e], dl[e])


def rest_base_kernel(me, faces, targets, bounds, v, pay, fb, rhs, a, dh, dl, own, late, base, acc):
    rest_kernel(me, faces, targets, bounds, v, pay, fb, own, late, acc)
    for e in range(E):
        base[e] = rhs[e] - product(a[e], dh[e], dl[e])


def finish_rest(core, acc, pay, own, late):
    own[...] = acc[0:E]
    late[8:16] = acc[E : 2 * E].astype(bf16)
    late[16:18] = pay[pair(jnp.where(core == 0, 4, 3))]


def rest_kernel(me, faces, targets, bounds, v, pay, fb, own, late, acc):
    add_faces(bounds[0], bounds[1], v, fb, faces, targets, acc)
    finish_rest(lax.bitwise_and(me[0], 1), acc, pay, own, late)


def bundle_kernel(me, got, pay, near_in, near, skip):
    core = lax.bitwise_and(me[0], 1)
    near[10:12] = got[pair(jnp.where(core == 0, 1, 0))]
    near[14:16] = got[pair(jnp.where(core == 0, 0, 1))]
    skip[0:2] = jnp.where(core == 0, got[4:6], pay[0:2])
    skip[2:4] = got[6:8]
    skip[4:6] = got[4:6]


def take(total, donor, k, row, live=None):
    for c in range(2):
        target = donor[2 * k + c]
        if live is not None:
            target = jnp.where(live, target, E)
        total[target] -= row[c].astype(f32)


def relay_kernel(near, skip, after, late_in, late):
    late[0:4] = near[12:16]
    late[4:8] = skip[0:4]


def gather_kernel(me, donor, own, near, skip, half, out, total):
    core = lax.bitwise_and(me[0], 1)
    total[0:E] = own[...] + near[0:E].astype(f32)
    total[E] = jnp.zeros((R, B), f32)
    take(total, donor, jnp.where(core == 0, 4, 3), near[8:10])
    take(total, donor, jnp.where(core == 0, 5, 2), near[10:12])
    take(total, donor, 7, half[...])
    take(total, donor, 0, skip[4:6], core == 0)
    out[...] = total[0:E]


def settle(core, donor, total_in, late, total):
    total[0:E] = total_in[...] + late[8:16].astype(f32)
    total[E] = jnp.zeros((R, B), f32)
    take(total, donor, jnp.where(core == 0, 2, 5), late[0:2])
    take(total, donor, jnp.where(core == 0, 1, 6), late[2:4])
    take(total, donor, jnp.where(core == 0, 6, 0), late[4:6])
    take(total, donor, 1, late[6:8], core == 1)
    take(total, donor, jnp.where(core == 0, 3, 4), late[16:18])


def update_kernel(with_sum, keep_x, me, donor, rows, scales, base, *refs):
    if with_sum:
        a_in, *refs = refs
    total_in, late, ph, plo, out, v_out, pay, early, half, total, v = refs
    core = lax.bitwise_and(me[0], 1)
    settle(core, donor, total_in, late, total)
    for e in range(E):
        x = base[e] - total[e]
        u = product(x, ph[e], plo[e])
        if with_sum:
            u = u + a_in[e]
        v[e] = u
        v_out[e] = u.astype(bf16)
        out[e] = x if keep_x else u
    emit_pairs(core, v, rows, scales, pay, early, half)


def last_kernel(me, donor, base, a_in, total_in, late, ph, plo, out, total):
    settle(lax.bitwise_and(me[0], 1), donor, total_in, late, total)
    for e in range(E):
        out[e] = a_in[e] + product(base[e] - total[e], ph[e], plo[e])


VALUE = jax.ShapeDtypeStruct((E, R, B), f32)
BLOCK = (E, B, B)


def rows_of(count):
    return pltpu.VMEM((count, R, B), bf16)


def call(kernel, name, ins, outs, scratch=(), **options):
    return pl.pallas_call(
        kernel,
        in_specs=ins,
        out_specs=[SM if o.memory_space == pltpu.SMEM else VM for o in outs],
        out_shape=outs,
        scratch_shapes=scratch,
        compiler_params=pltpu.CompilerParams(vmem_limit_bytes=20 * MIB),
        name=name,
        **options,
    )


def pin(x, space=pltpu.VMEM):
    return pltpu.with_memory_space_constraint(x, space)


def swap(x):
    return lax.ppermute(x, "dom", [(s, s ^ 1) for s in range(N)])


def near_swap(x):
    return lax.ppermute(x, "dom", [(s, (s + (1 if s % 2 else -1)) % N) for s in range(N)])


def skip_shift(x):
    return lax.ppermute(x, "dom", [(s, (s + (-5 if s % 2 else 5)) % N) for s in range(N)])


def half_swap(x):
    return lax.ppermute(x, "dom", [(s, s ^ 64) for s in range(N)])


def local(rhs, diag_block, precond, face_block, face_nbr, pair_recv_elem, pair_donor_dev,
          pair_donor_elem, pair_weight, fringe_count):
    me = lax.axis_index("dom").astype(jnp.int32).reshape(1)
    donor = pair_donor_elem
    value = pltpu.VMEM((E, R, B), f32)
    total = pltpu.VMEM((E + 1, R, B), f32)
    acc = pltpu.VMEM((2 * E + 1, R, B), f32)
    sent = [rows_of(E), rows_of(PAIRS), rows_of(8), rows_of(2)]
    hbm = lambda x: pin(x, pltpu.HBM)
    smem = lambda x: pin(x, pltpu.SMEM)
    table = lambda n, dtype=jnp.int32: pltpu.SMEM((n,), dtype)

    faces, targets, bounds, rows, scales, ph, plo, fb, v, pay, early, half = call(
        start_kernel, "start", [SM] * 6 + [VM, ANY, ANY],
        [table(LIST), table(LIST), table(2), table(PAIRS), table(PAIRS, f32),
         pltpu.VMEM(BLOCK, bf16), pltpu.VMEM(BLOCK, bf16), pltpu.VMEM((E * FACES, B, B), bf16)] + sent,
        [pltpu.VMEM(BLOCK, f32), pltpu.VMEM((AHEAD, FACES, B, B), f32), value,
         pltpu.SemaphoreType.DMA((E,)), pltpu.SemaphoreType.DMA((AHEAD,))],
    )(me, hbm(face_nbr), hbm(pair_recv_elem), hbm(pair_donor_dev.reshape(-1)), hbm(pair_weight), fringe_count,
      hbm(rhs), hbm(precond), hbm(face_block))
    faces, targets, bounds = smem(faces), smem(targets), smem(bounds)
    rows, scales, ph, plo = smem(rows), smem(scales), pin(ph), pin(plo)

    got = swap(early)
    stream = [acc, pltpu.VMEM((DEPTH, GROUP, B, B), f32), pltpu.SemaphoreType.DMA((DEPTH, GROUP))]
    fb_shape = pltpu.VMEM((E * FACES, B, B), bf16)
    near, fb = call(
        load_kernel, "load", [SM] * 4 + [VM] * 3 + [ANY], [rows_of(16), fb_shape], stream,
        input_output_aliases={6: 1},
    )(me, faces, targets, bounds, pin(v), pin(pay), pin(fb), hbm(face_block))

    def exchange(v, near, half, pay, got, fb, kernel=rest_kernel, more=(), outs=(), scratch=(acc,), **options):
        near, skip = call(
            bundle_kernel, "bundle", [SM, VM, VM, VM], [rows_of(16), rows_of(6)], input_output_aliases={3: 0},
        )(me, pin(got), pin(pay), pin(near))
        near, skip, half = near_swap(near), skip_shift(skip), half_swap(half)
        own, late, *others = call(
            kernel, "rest", [SM] * 4 + [VM] * 3 + [ANY if x is face_block else VM for x in more],
            [value, rows_of(18), *outs], scratch, **options,
        )(me, faces, targets, bounds, pin(v), pin(pay), pin(fb), *[hbm(x) if x is face_block else pin(x) for x in more])
        late = call(
            relay_kernel, "relay", [VM, VM, ANY, VM], [rows_of(18)], input_output_aliases={3: 0},
        )(pin(near), pin(skip), pin(half), pin(late))[0]
        sums = call(
            gather_kernel, "gather", [SM, SM] + [VM] * 4, [value], [total],
        )(me, donor, pin(own), pin(near), pin(skip), pin(half))[0]
        return (sums, swap(late)), *others

    def step(base, a, keep_x, sums, late, *rest):
        args = [pin(base)] + ([pin(a)] if a is not None else [])
        out, v, pay, early, half = call(
            lambda *refs: update_kernel(a is not None, keep_x, *refs), "update", [SM] * 4 + [VM] * (len(args) + 4),
            [value] + sent, [total, value],
        )(me, donor, rows, scales, *args, pin(sums), pin(late), ph, plo)
        got = swap(early)
        near = call(
            near_kernel, "near", [SM] * 4 + [VM] * 3, [rows_of(16)], [acc],
        )(me, faces, targets, bounds, pin(v), pin(pay), fb)[0]
        if rest:
            kernel, more, outs = rest
            return out, *exchange(v, near, half, pay, got, fb, kernel, (rhs, out, *more), [value, *outs])
        return out, *exchange(v, near, half, pay, got, fb)

    sums, fb = exchange(
        v, near, half, pay, got, fb, rest_load_kernel, (face_block,), [fb_shape], stream, input_output_aliases={6: 2})
    fb = pin(fb)
    blocks = [pltpu.VMEM(BLOCK, bf16)] * 2
    a1, sums, base, dh, dl = step(rhs, None, False, *sums, rest_split_kernel, (diag_block,), blocks)
    r1, sums = step(base, None, True, *sums)
    a2, sums, base = step(r1, a1, False, *sums, rest_base_kernel, (dh, dl), [])
    r2, sums = step(base, None, True, *sums)
    return pl.pallas_call(
        last_kernel, in_specs=[SM, SM] + [VM] * 6, out_specs=VM, out_shape=VALUE, scratch_shapes=[total],
        compiler_params=pltpu.CompilerParams(vmem_limit_bytes=20 * MIB), name="last",
    )(me, donor, pin(r2), pin(a2), *map(pin, sums), ph, plo)


def solution(mesh):
    dom = P("dom")
    return jax.shard_map(local, mesh=mesh, in_specs=(dom,) * 10, out_specs=dom, check_vma=False)
```

```python
import jax
import jax.numpy as jnp
from jax import lax
from jax.experimental import pallas as pl
from jax.experimental.pallas import tpu as pltpu
from jax.sharding import PartitionSpec as P

E = 8
R = 16
B = 320
FACES = 6
PAIRS = 16
N = 128
GROUP = 8
LIST = E * FACES + 2 * GROUP
AHEAD = 1
DEPTH = 3
MIB = 1024 * 1024
f32 = jnp.float32
bf16 = jnp.bfloat16

VM = pl.BlockSpec(memory_space=pltpu.VMEM)
SM = pl.BlockSpec(memory_space=pltpu.SMEM)
ANY = pl.BlockSpec(memory_space=pl.ANY)


def dot(a, b):
    return jnp.dot(a, b, preferred_element_type=f32)


def halves(x):
    high = x.astype(bf16)
    return high, (x - high.astype(f32)).astype(bf16)


def product(x, high, low):
    x_high, x_low = halves(x)
    both = dot(jnp.concatenate([x_high, x_low], axis=0), high)
    return both[:R] + both[R:] + dot(x_high, low)


def late_product(x, high):
    x_high, x_low = halves(x)
    both = dot(jnp.concatenate([x_high, x_low], axis=0), high)
    return both[:R] + both[R:]


def pair(k):
    return pl.ds(2 * k, 2)


def fill_tables(me, nbr, recv, dev, weight, count, faces, targets, bounds, rows, scales):
    core = lax.bitwise_and(me, 1)
    near_side = jnp.where(core == 0, 0, 2)
    for i in range(LIST):
        faces[i] = 0
        targets[i] = 2 * E
    kinds = []
    total = jnp.int32(0)
    for e in range(E):
        for f in range(FACES):
            n = nbr[e, f]
            side = lax.bitwise_and(lax.shift_right_logical(n, 3) - me + 129, 127)
            near = side == near_side
            row = lax.bitwise_and(n, 7)
            kinds.append((near, jnp.where(near | (side == 1), row, row + E)))
            total = total + near.astype(jnp.int32)
    groups = lax.div(total + GROUP - 1, GROUP)
    bounds[0] = groups
    bounds[1] = groups + lax.div(E * FACES - total + GROUP - 1, GROUP)
    first, second = jnp.int32(0), groups * GROUP
    for i, (near, row) in enumerate(kinds):
        at = jnp.where(near, first, second)
        faces[at] = i
        targets[at] = row
        step = near.astype(jnp.int32)
        first, second = first + step, second + 1 - step
    counts = [jnp.int32(0)] * 8
    for p in range(PAIRS):
        distance = lax.bitwise_and(dev[p] - me + 128, 127)
        bucket = jnp.where(distance <= 4, distance + 3, distance - 124)
        bucket = jnp.where(distance == 64, 7, bucket)
        position = jnp.int32(0)
        for k in range(8):
            hit = (bucket == k).astype(jnp.int32)
            position = position + hit * counts[k]
            counts[k] = counts[k] + hit
        rows[bucket * 2 + position] = recv[p]
        scales[bucket * 2 + position] = jnp.where(p < count[0], weight[p], f32(0.0))


def emit_pairs(core, v, rows, scales, pay, early, half):
    for slot in range(PAIRS):
        pay[slot] = (scales[slot] * v[rows[slot]]).astype(bf16)
    half[...] = pay[14:16]
    for j, (k0, k1) in enumerate(((5, 1), (6, 2), (0, 6), (1, 6))):
        early[2 * j : 2 * j + 2] = pay[pair(jnp.where(core == 0, k0, k1))]


def add_faces(low, high, v, fb, faces, targets, acc):
    acc[...] = jnp.zeros_like(acc)

    def group(g, carry):
        terms = []
        for j in range(GROUP):
            face = faces[g * GROUP + j]
            terms.append(dot(v[lax.div(face, FACES)], fb[face]))
        for j in range(GROUP):
            acc[targets[g * GROUP + j]] += terms[j]
        return carry

    lax.fori_loop(low, high, group, 0)


def finish_near(core, acc, pay, near):
    near[0:E] = acc[0:E].astype(bf16)
    near[8:10] = pay[pair(jnp.where(core == 0, 3, 4))]
    near[12:14] = pay[pair(jnp.where(core == 0, 2, 5))]


def start_kernel(me, nbr, recv, dev, weight, count, rhs, precond, face,
                 faces, targets, bounds, rows, scales, ph, plo, fb, v_out, pay, early, half,
                 pbuf, fbuf, v, psem, fsem):
    def fetch(e):
        return pltpu.make_async_copy(precond.at[e], pbuf.at[e], psem.at[e])

    def fetch_face(e):
        return pltpu.make_async_copy(face.at[e], fbuf.at[e], fsem.at[e])

    for e in range(E):
        fetch(e).start()
    for e in range(AHEAD):
        fetch_face(e).start()
    fill_tables(me[0], nbr, recv, dev, weight, count, faces, targets, bounds, rows, scales)
    for e in range(E):
        fetch(e).wait()
        high, low = halves(pbuf[e])
        ph[e] = high
        plo[e] = low
        v[e] = product(rhs[e], high, low)
        v_out[e] = v[e].astype(bf16)
    emit_pairs(lax.bitwise_and(me[0], 1), v, rows, scales, pay, early, half)
    for e in range(AHEAD):
        fetch_face(e).wait()
        for f in range(FACES):
            fb[e * FACES + f] = fbuf[e, f].astype(bf16)


def add_streamed(low, high, v, face, fb, faces, targets, acc, fbuf, sems):
    acc[...] = jnp.zeros_like(acc)

    def each(g, act):
        slot = lax.rem(g - low, DEPTH)
        for j in range(GROUP):
            i = g * GROUP + j
            block = faces[i]

            @pl.when((targets[i] < 2 * E) & (block >= AHEAD * FACES))
            def _():
                source = face.at[lax.div(block, FACES), lax.rem(block, FACES)]
                act(block, fbuf.at[slot, j], pltpu.make_async_copy(source, fbuf.at[slot, j], sems.at[slot, j]))

    def start(block, held, copy):
        copy.start()

    def settle(block, held, copy):
        copy.wait()
        fb[block] = held[...].astype(bf16)

    for ahead in range(DEPTH):
        @pl.when(low + ahead < high)
        def _():
            each(low + ahead, start)

    def group(g, carry):
        each(g, settle)

        @pl.when(g + DEPTH < high)
        def _():
            each(g + DEPTH, start)

        terms = []
        for j in range(GROUP):
            block = faces[g * GROUP + j]
            terms.append(dot(v[lax.div(block, FACES)], fb[block]))
        for j in range(GROUP):
            acc[targets[g * GROUP + j]] += terms[j]
        return carry

    lax.fori_loop(low, high, group, 0)


def load_kernel(me, faces, targets, bounds, v, pay, fb_in, face, near, fb, acc, fbuf, sems):
    add_streamed(0, bounds[0], v, face, fb, faces, targets, acc, fbuf, sems)
    finish_near(lax.bitwise_and(me[0], 1), acc, pay, near)


def near_kernel(me, faces, targets, bounds, v, pay, fb, near, acc):
    add_faces(0, bounds[0], v, fb, faces, targets, acc)
    finish_near(lax.bitwise_and(me[0], 1), acc, pay, near)


def rest_load_kernel(me, faces, targets, bounds, v, pay, fb_in, face, own, late, fb, acc, fbuf, sems):
    add_streamed(bounds[0], bounds[1], v, face, fb, faces, targets, acc, fbuf, sems)
    finish_rest(lax.bitwise_and(me[0], 1), acc, pay, own, late)


def rest_split_kernel(me, faces, targets, bounds, v, pay, fb, rhs, a, diag, own, late, base, dh, dl, acc):
    rest_kernel(me, faces, targets, bounds, v, pay, fb, own, late, acc)
    for e in range(E):
        dh[e], dl[e] = halves(diag[e])
        base[e] = rhs[e] - product(a[e], dh[e], dl[e])


def rest_base_kernel(me, faces, targets, bounds, v, pay, fb, rhs, a, dh, dl, own, late, base, acc):
    rest_kernel(me, faces, targets, bounds, v, pay, fb, own, late, acc)
    for e in range(E):
        base[e] = rhs[e] - product(a[e], dh[e], dl[e])


def finish_rest(core, acc, pay, own, late):
    own[...] = acc[0:E]
    late[8:16] = acc[E : 2 * E].astype(bf16)
    late[16:18] = pay[pair(jnp.where(core == 0, 4, 3))]


def rest_kernel(me, faces, targets, bounds, v, pay, fb, own, late, acc):
    add_faces(bounds[0], bounds[1], v, fb, faces, targets, acc)
    finish_rest(lax.bitwise_and(me[0], 1), acc, pay, own, late)


def bundle_kernel(me, got, pay, near_in, near, skip):
    core = lax.bitwise_and(me[0], 1)
    near[10:12] = got[pair(jnp.where(core == 0, 1, 0))]
    near[14:16] = got[pair(jnp.where(core == 0, 0, 1))]
    skip[0:2] = jnp.where(core == 0, got[4:6], pay[0:2])
    skip[2:4] = got[6:8]
    skip[4:6] = got[4:6]


def take(total, donor, k, row, live=None):
    for c in range(2):
        target = donor[2 * k + c]
        if live is not None:
            target = jnp.where(live, target, E)
        total[target] -= row[c].astype(f32)


def relay_kernel(near, skip, after, late_in, late):
    late[0:4] = near[12:16]
    late[4:8] = skip[0:4]


def gather_kernel(me, donor, base, own, near, skip, half, ph, plo, x_out, u_out, total):
    core = lax.bitwise_and(me[0], 1)
    total[0:E] = own[...] + near[0:E].astype(f32)
    total[E] = jnp.zeros((R, B), f32)
    take(total, donor, jnp.where(core == 0, 4, 3), near[8:10])
    take(total, donor, jnp.where(core == 0, 5, 2), near[10:12])
    take(total, donor, 7, half[...])
    take(total, donor, 0, skip[4:6], core == 0)
    for e in range(E):
        x = base[e] - total[e]
        x_out[e] = x
        u_out[e] = product(x, ph[e], plo[e])


def settle(core, donor, late, total):
    total[0:E] = late[8:16].astype(f32)
    total[E] = jnp.zeros((R, B), f32)
    take(total, donor, jnp.where(core == 0, 2, 5), late[0:2])
    take(total, donor, jnp.where(core == 0, 1, 6), late[2:4])
    take(total, donor, jnp.where(core == 0, 6, 0), late[4:6])
    take(total, donor, 1, late[6:8], core == 1)
    take(total, donor, jnp.where(core == 0, 3, 4), late[16:18])


def update_kernel(with_sum, keep_x, me, donor, rows, scales, *refs):
    if with_sum:
        a_in, *refs = refs
    x, u_in, late, ph, out, v_out, pay, early, half, total, v = refs
    core = lax.bitwise_and(me[0], 1)
    settle(core, donor, late, total)
    for e in range(E):
        u = u_in[e] - late_product(total[e], ph[e])
        if with_sum:
            u = u + a_in[e]
        v[e] = u
        v_out[e] = u.astype(bf16)
        out[e] = x[e] - total[e] if keep_x else u
    emit_pairs(core, v, rows, scales, pay, early, half)


def last_kernel(me, donor, a_in, u_in, late, ph, out, total):
    settle(lax.bitwise_and(me[0], 1), donor, late, total)
    for e in range(E):
        out[e] = a_in[e] + (u_in[e] - late_product(total[e], ph[e]))


VALUE = jax.ShapeDtypeStruct((E, R, B), f32)
BLOCK = (E, B, B)


def rows_of(count):
    return pltpu.VMEM((count, R, B), bf16)


def call(kernel, name, ins, outs, scratch=(), **options):
    return pl.pallas_call(
        kernel,
        in_specs=ins,
        out_specs=[SM if o.memory_space == pltpu.SMEM else VM for o in outs],
        out_shape=outs,
        scratch_shapes=scratch,
        compiler_params=pltpu.CompilerParams(vmem_limit_bytes=20 * MIB),
        name=name,
        **options,
    )


def pin(x, space=pltpu.VMEM):
    return pltpu.with_memory_space_constraint(x, space)


def swap(x):
    return lax.ppermute(x, "dom", [(s, s ^ 1) for s in range(N)])


def near_swap(x):
    return lax.ppermute(x, "dom", [(s, (s + (1 if s % 2 else -1)) % N) for s in range(N)])


def skip_shift(x):
    return lax.ppermute(x, "dom", [(s, (s + (-5 if s % 2 else 5)) % N) for s in range(N)])


def half_swap(x):
    return lax.ppermute(x, "dom", [(s, s ^ 64) for s in range(N)])


def local(rhs, diag_block, precond, face_block, face_nbr, pair_recv_elem, pair_donor_dev,
          pair_donor_elem, pair_weight, fringe_count):
    me = lax.axis_index("dom").astype(jnp.int32).reshape(1)
    donor = pair_donor_elem
    value = pltpu.VMEM((E, R, B), f32)
    total = pltpu.VMEM((E + 1, R, B), f32)
    acc = pltpu.VMEM((2 * E + 1, R, B), f32)
    sent = [rows_of(E), rows_of(PAIRS), rows_of(8), rows_of(2)]
    hbm = lambda x: pin(x, pltpu.HBM)
    smem = lambda x: pin(x, pltpu.SMEM)
    table = lambda n, dtype=jnp.int32: pltpu.SMEM((n,), dtype)

    faces, targets, bounds, rows, scales, ph, plo, fb, v, pay, early, half = call(
        start_kernel, "start", [SM] * 6 + [VM, ANY, ANY],
        [table(LIST), table(LIST), table(2), table(PAIRS), table(PAIRS, f32),
         pltpu.VMEM(BLOCK, bf16), pltpu.VMEM(BLOCK, bf16), pltpu.VMEM((E * FACES, B, B), bf16)] + sent,
        [pltpu.VMEM(BLOCK, f32), pltpu.VMEM((AHEAD, FACES, B, B), f32), value,
         pltpu.SemaphoreType.DMA((E,)), pltpu.SemaphoreType.DMA((AHEAD,))],
    )(me, hbm(face_nbr), hbm(pair_recv_elem), hbm(pair_donor_dev.reshape(-1)), hbm(pair_weight), fringe_count,
      hbm(rhs), hbm(precond), hbm(face_block))
    faces, targets, bounds = smem(faces), smem(targets), smem(bounds)
    rows, scales, ph, plo = smem(rows), smem(scales), pin(ph), pin(plo)

    got = swap(early)
    stream = [acc, pltpu.VMEM((DEPTH, GROUP, B, B), f32), pltpu.SemaphoreType.DMA((DEPTH, GROUP))]
    fb_shape = pltpu.VMEM((E * FACES, B, B), bf16)
    near, fb = call(
        load_kernel, "load", [SM] * 4 + [VM] * 3 + [ANY], [rows_of(16), fb_shape], stream,
        input_output_aliases={6: 1},
    )(me, faces, targets, bounds, pin(v), pin(pay), pin(fb), hbm(face_block))

    def exchange(base, v, near, half, pay, got, fb, kernel=rest_kernel, more=(), outs=(), scratch=(acc,), **options):
        near, skip = call(
            bundle_kernel, "bundle", [SM, VM, VM, VM], [rows_of(16), rows_of(6)], input_output_aliases={3: 0},
        )(me, pin(got), pin(pay), pin(near))
        near, skip, half = near_swap(near), skip_shift(skip), half_swap(half)
        own, late, *others = call(
            kernel, "rest", [SM] * 4 + [VM] * 3 + [ANY if x is face_block else VM for x in more],
            [value, rows_of(18), *outs], scratch, **options,
        )(me, faces, targets, bounds, pin(v), pin(pay), pin(fb), *[hbm(x) if x is face_block else pin(x) for x in more])
        late = call(
            relay_kernel, "relay", [VM, VM, ANY, VM], [rows_of(18)], input_output_aliases={3: 0},
        )(pin(near), pin(skip), pin(half), pin(late))[0]
        if base is None:
            base, *others = others
        x, u = call(
            gather_kernel, "gather", [SM, SM] + [VM] * 7, [value, value], [total],
        )(me, donor, *map(pin, (base, own, near, skip, half)), ph, plo)
        return (x, u, swap(late)), *others

    def step(a, keep_x, x, u, late, *rest):
        args = [pin(a)] if a is not None else []
        out, v, pay, early, half = call(
            lambda *refs: update_kernel(a is not None, keep_x, *refs), "update", [SM] * 4 + [VM] * (len(args) + 4),
            [value] + sent, [total, value],
        )(me, donor, rows, scales, *args, pin(x), pin(u), pin(late), ph)
        got = swap(early)
        near = call(
            near_kernel, "near", [SM] * 4 + [VM] * 3, [rows_of(16)], [acc],
        )(me, faces, targets, bounds, pin(v), pin(pay), fb)[0]
        if rest:
            kernel, more, outs = rest
            return out, *exchange(None, v, near, half, pay, got, fb, kernel, (rhs, out, *more), [value, *outs])
        return out, *exchange(out, v, near, half, pay, got, fb)

    sums, fb = exchange(
        rhs, v, near, half, pay, got, fb, rest_load_kernel, (face_block,), [fb_shape], stream,
        input_output_aliases={6: 2})
    fb = pin(fb)
    blocks = [pltpu.VMEM(BLOCK, bf16)] * 2
    a1, sums, dh, dl = step(None, False, *sums, rest_split_kernel, (diag_block,), blocks)
    _, sums = step(None, True, *sums)
    a2, sums = step(a1, False, *sums, rest_base_kernel, (dh, dl), [])
    _, sums = step(None, True, *sums)
    _, u, late = sums
    return pl.pallas_call(
        last_kernel, in_specs=[SM, SM] + [VM] * 4, out_specs=VM, out_shape=VALUE, scratch_shapes=[total],
        compiler_params=pltpu.CompilerParams(vmem_limit_bytes=20 * MIB), name="last",
    )(me, donor, pin(a2), pin(u), pin(late), ph)


def solution(mesh):
    dom = P("dom")
    return jax.shard_map(local, mesh=mesh, in_specs=(dom,) * 10, out_specs=dom, check_vma=False)
```

```python
import functools

import jax
import jax.numpy as jnp
from jax import lax
from jax.experimental import pallas as pl
from jax.experimental.pallas import tpu as pltpu
from jax.sharding import PartitionSpec as P

E = 8
R = 16
B = 320
FACES = 6
PAIRS = 16
N = 128
GROUP = 8
LIST = E * FACES + 2 * GROUP
AHEAD = 1
DEPTH = 3
MIB = 1024 * 1024
f32 = jnp.float32
bf16 = jnp.bfloat16

VM = pl.BlockSpec(memory_space=pltpu.VMEM)
SM = pl.BlockSpec(memory_space=pltpu.SMEM)
ANY = pl.BlockSpec(memory_space=pl.ANY)


def dot(a, b):
    return jnp.dot(a, b, preferred_element_type=f32)


def halves(x):
    high = x.astype(bf16)
    return high, (x - high.astype(f32)).astype(bf16)


def product(x, high, low):
    x_high, x_low = halves(x)
    both = dot(jnp.concatenate([x_high, x_low], axis=0), high)
    return both[:R] + both[R:] + dot(x_high, low)


def late_product(x, high):
    x_high, x_low = halves(x)
    both = dot(jnp.concatenate([x_high, x_low], axis=0), high)
    return both[:R] + both[R:]


def pair(k):
    return pl.ds(2 * k, 2)


def fill_tables(me, nbr, recv, dev, weight, count, faces, targets, bounds, rows, scales):
    core = lax.bitwise_and(me, 1)
    near_side = jnp.where(core == 0, 0, 2)
    for i in range(LIST):
        faces[i] = 0
        targets[i] = 2 * E
    kinds = []
    total = jnp.int32(0)
    for e in range(E):
        for f in range(FACES):
            n = nbr[e, f]
            side = lax.bitwise_and(lax.shift_right_logical(n, 3) - me + 129, 127)
            near = side == near_side
            row = lax.bitwise_and(n, 7)
            kinds.append((near, jnp.where(near | (side == 1), row, row + E)))
            total = total + near.astype(jnp.int32)
    groups = lax.div(total + GROUP - 1, GROUP)
    bounds[0] = groups
    bounds[1] = groups + lax.div(E * FACES - total + GROUP - 1, GROUP)
    first, second = jnp.int32(0), groups * GROUP
    for i, (near, row) in enumerate(kinds):
        at = jnp.where(near, first, second)
        faces[at] = i
        targets[at] = row
        step = near.astype(jnp.int32)
        first, second = first + step, second + 1 - step
    counts = [jnp.int32(0)] * 8
    for p in range(PAIRS):
        distance = lax.bitwise_and(dev[p] - me + 128, 127)
        bucket = jnp.where(distance <= 4, distance + 3, distance - 124)
        bucket = jnp.where(distance == 64, 7, bucket)
        position = jnp.int32(0)
        for k in range(8):
            hit = (bucket == k).astype(jnp.int32)
            position = position + hit * counts[k]
            counts[k] = counts[k] + hit
        rows[bucket * 2 + position] = recv[p]
        scales[bucket * 2 + position] = jnp.where(p < count[0], weight[p], f32(0.0))


def emit_pairs(core, v, rows, scales, pay, early, half):
    for slot in range(PAIRS):
        pay[slot] = (scales[slot] * v[rows[slot]]).astype(bf16)
    half[...] = pay[14:16]
    for j, (k0, k1) in enumerate(((5, 1), (6, 2), (0, 6), (1, 6))):
        early[2 * j : 2 * j + 2] = pay[pair(jnp.where(core == 0, k0, k1))]


def add_faces(low, high, v, fb, faces, targets, acc):
    acc[...] = jnp.zeros_like(acc)

    def group(g, carry):
        terms = []
        for j in range(GROUP):
            face = faces[g * GROUP + j]
            terms.append(dot(v[lax.div(face, FACES)], fb[face]))
        for j in range(GROUP):
            acc[targets[g * GROUP + j]] += terms[j]
        return carry

    lax.fori_loop(low, high, group, 0)


def finish_near(core, acc, pay, near):
    near[0:E] = acc[0:E].astype(bf16)
    near[8:10] = pay[pair(jnp.where(core == 0, 3, 4))]
    near[12:14] = pay[pair(jnp.where(core == 0, 2, 5))]


def start_kernel(me, nbr, recv, dev, weight, count, rhs, precond, face,
                 faces, targets, bounds, rows, scales, ph, plo, fb, v_out, pay, early, half,
                 pbuf, fbuf, v, psem, fsem):
    def fetch(e):
        return pltpu.make_async_copy(precond.at[e], pbuf.at[e], psem.at[e])

    def fetch_face(e):
        return pltpu.make_async_copy(face.at[e], fbuf.at[e], fsem.at[e])

    for e in range(E):
        fetch(e).start()
    for e in range(AHEAD):
        fetch_face(e).start()
    fill_tables(me[0], nbr, recv, dev, weight, count, faces, targets, bounds, rows, scales)
    for e in range(E):
        fetch(e).wait()
        high, low = halves(pbuf[e])
        ph[e] = high
        plo[e] = low
        v[e] = product(rhs[e], high, low)
        v_out[e] = v[e].astype(bf16)
    emit_pairs(lax.bitwise_and(me[0], 1), v, rows, scales, pay, early, half)
    for e in range(AHEAD):
        fetch_face(e).wait()
        for f in range(FACES):
            fb[e * FACES + f] = fbuf[e, f].astype(bf16)


def add_streamed(low, high, v, face, fb, faces, targets, acc, fbuf, sems):
    acc[...] = jnp.zeros_like(acc)

    def each(g, act):
        slot = lax.rem(g - low, DEPTH)
        for j in range(GROUP):
            i = g * GROUP + j
            block = faces[i]

            @pl.when((targets[i] < 2 * E) & (block >= AHEAD * FACES))
            def _():
                source = face.at[lax.div(block, FACES), lax.rem(block, FACES)]
                act(block, fbuf.at[slot, j], pltpu.make_async_copy(source, fbuf.at[slot, j], sems.at[slot, j]))

    def start(block, held, copy):
        copy.start()

    def settle(block, held, copy):
        copy.wait()
        fb[block] = held[...].astype(bf16)

    for ahead in range(DEPTH):
        @pl.when(low + ahead < high)
        def _():
            each(low + ahead, start)

    def group(g, carry):
        each(g, settle)

        @pl.when(g + DEPTH < high)
        def _():
            each(g + DEPTH, start)

        terms = []
        for j in range(GROUP):
            block = faces[g * GROUP + j]
            terms.append(dot(v[lax.div(block, FACES)], fb[block]))
        for j in range(GROUP):
            acc[targets[g * GROUP + j]] += terms[j]
        return carry

    lax.fori_loop(low, high, group, 0)


def load_kernel(me, faces, targets, bounds, v, pay, fb_in, face, near, fb, acc, fbuf, sems):
    add_streamed(0, bounds[0], v, face, fb, faces, targets, acc, fbuf, sems)
    finish_near(lax.bitwise_and(me[0], 1), acc, pay, near)


def near_kernel(me, faces, targets, bounds, v, pay, fb, near, acc):
    add_faces(0, bounds[0], v, fb, faces, targets, acc)
    finish_near(lax.bitwise_and(me[0], 1), acc, pay, near)


def rest_load_kernel(me, faces, targets, bounds, v, pay, fb_in, face, own, late, fb, acc, fbuf, sems):
    add_streamed(bounds[0], bounds[1], v, face, fb, faces, targets, acc, fbuf, sems)
    finish_rest(lax.bitwise_and(me[0], 1), acc, pay, own, late)


def rest_split_kernel(me, faces, targets, bounds, v, pay, fb, rhs, a, diag, own, late, base, dh, dl, acc):
    rest_kernel(me, faces, targets, bounds, v, pay, fb, own, late, acc)
    for e in range(E):
        dh[e], dl[e] = halves(diag[e])
        base[e] = rhs[e] - product(a[e], dh[e], dl[e])


def rest_base_kernel(me, faces, targets, bounds, v, pay, fb, rhs, a, dh, dl, own, late, base, acc):
    rest_kernel(me, faces, targets, bounds, v, pay, fb, own, late, acc)
    for e in range(E):
        base[e] = rhs[e] - product(a[e], dh[e], dl[e])


def finish_rest(core, acc, pay, own, late):
    own[...] = acc[0:E]
    late[8:16] = acc[E : 2 * E].astype(bf16)
    late[16:18] = pay[pair(jnp.where(core == 0, 4, 3))]


def rest_kernel(me, faces, targets, bounds, v, pay, fb, own, late, acc):
    add_faces(bounds[0], bounds[1], v, fb, faces, targets, acc)
    finish_rest(lax.bitwise_and(me[0], 1), acc, pay, own, late)


def bundle_kernel(me, got, pay, near_in, near, skip):
    core = lax.bitwise_and(me[0], 1)
    near[10:12] = got[pair(jnp.where(core == 0, 1, 0))]
    near[14:16] = got[pair(jnp.where(core == 0, 0, 1))]
    skip[0:2] = jnp.where(core == 0, got[4:6], pay[0:2])
    skip[2:4] = got[6:8]
    skip[4:6] = got[4:6]


def take(total, donor, k, row, live=None):
    for c in range(2):
        target = donor[2 * k + c]
        if live is not None:
            target = jnp.where(live, target, E)
        total[target] -= row[c].astype(f32)


def relay_kernel(near, skip, after, late_in, late):
    late[0:4] = near[12:16]
    late[4:8] = skip[0:4]


def gather_kernel(keep_x, me, donor, base, own, near, skip, half, ph, plo, *refs):
    *x_out, u_out, total = refs
    core = lax.bitwise_and(me[0], 1)
    total[0:E] = own[...] + near[0:E].astype(f32)
    total[E] = jnp.zeros((R, B), f32)
    take(total, donor, jnp.where(core == 0, 4, 3), near[8:10])
    take(total, donor, jnp.where(core == 0, 5, 2), near[10:12])
    take(total, donor, 7, half[...])
    take(total, donor, 0, skip[4:6], core == 0)
    for e in range(E):
        x = base[e] - total[e]
        if keep_x:
            x_out[0][e] = x
        u_out[e] = product(x, ph[e], plo[e])


def settle(core, donor, late, total):
    total[0:E] = late[8:16].astype(f32)
    total[E] = jnp.zeros((R, B), f32)
    take(total, donor, jnp.where(core == 0, 2, 5), late[0:2])
    take(total, donor, jnp.where(core == 0, 1, 6), late[2:4])
    take(total, donor, jnp.where(core == 0, 6, 0), late[4:6])
    take(total, donor, 1, late[6:8], core == 1)
    take(total, donor, jnp.where(core == 0, 3, 4), late[16:18])


def update_kernel(with_sum, keep_x, me, donor, rows, scales, *refs):
    if with_sum:
        a_in, *refs = refs
    if keep_x:
        x, *refs = refs
    u_in, late, ph, out, v_out, pay, early, half, total, v = refs
    core = lax.bitwise_and(me[0], 1)
    settle(core, donor, late, total)
    for e in range(E):
        u = u_in[e] - late_product(total[e], ph[e])
        if with_sum:
            u = u + a_in[e]
        v[e] = u
        v_out[e] = u.astype(bf16)
        out[e] = x[e] - total[e] if keep_x else u
    emit_pairs(core, v, rows, scales, pay, early, half)


def last_kernel(me, donor, a_in, u_in, late, ph, out, total):
    settle(lax.bitwise_and(me[0], 1), donor, late, total)
    for e in range(E):
        out[e] = a_in[e] + (u_in[e] - late_product(total[e], ph[e]))


VALUE = jax.ShapeDtypeStruct((E, R, B), f32)
BLOCK = (E, B, B)


def rows_of(count):
    return pltpu.VMEM((count, R, B), bf16)


def call(kernel, name, ins, outs, scratch=(), **options):
    return pl.pallas_call(
        kernel,
        in_specs=ins,
        out_specs=[SM if o.memory_space == pltpu.SMEM else VM for o in outs],
        out_shape=outs,
        scratch_shapes=scratch,
        compiler_params=pltpu.CompilerParams(vmem_limit_bytes=20 * MIB),
        name=name,
        **options,
    )


def pin(x, space=pltpu.VMEM):
    return pltpu.with_memory_space_constraint(x, space)


def swap(x):
    return lax.ppermute(x, "dom", [(s, s ^ 1) for s in range(N)])


def near_swap(x):
    return lax.ppermute(x, "dom", [(s, (s + (1 if s % 2 else -1)) % N) for s in range(N)])


def skip_shift(x):
    return lax.ppermute(x, "dom", [(s, (s + (-5 if s % 2 else 5)) % N) for s in range(N)])


def half_swap(x):
    return lax.ppermute(x, "dom", [(s, s ^ 64) for s in range(N)])


def local(rhs, diag_block, precond, face_block, face_nbr, pair_recv_elem, pair_donor_dev,
          pair_donor_elem, pair_weight, fringe_count):
    me = lax.axis_index("dom").astype(jnp.int32).reshape(1)
    donor = pair_donor_elem
    value = pltpu.VMEM((E, R, B), f32)
    total = pltpu.VMEM((E + 1, R, B), f32)
    acc = pltpu.VMEM((2 * E + 1, R, B), f32)
    sent = [rows_of(E), rows_of(PAIRS), rows_of(8), rows_of(2)]
    hbm = lambda x: pin(x, pltpu.HBM)
    smem = lambda x: pin(x, pltpu.SMEM)
    table = lambda n, dtype=jnp.int32: pltpu.SMEM((n,), dtype)

    faces, targets, bounds, rows, scales, ph, plo, fb, v, pay, early, half = call(
        start_kernel, "start", [SM] * 6 + [VM, ANY, ANY],
        [table(LIST), table(LIST), table(2), table(PAIRS), table(PAIRS, f32),
         pltpu.VMEM(BLOCK, bf16), pltpu.VMEM(BLOCK, bf16), pltpu.VMEM((E * FACES, B, B), bf16)] + sent,
        [pltpu.VMEM(BLOCK, f32), pltpu.VMEM((AHEAD, FACES, B, B), f32), value,
         pltpu.SemaphoreType.DMA((E,)), pltpu.SemaphoreType.DMA((AHEAD,))],
    )(me, hbm(face_nbr), hbm(pair_recv_elem), hbm(pair_donor_dev.reshape(-1)), hbm(pair_weight), fringe_count,
      hbm(rhs), hbm(precond), hbm(face_block))
    faces, targets, bounds = smem(faces), smem(targets), smem(bounds)
    rows, scales, ph, plo = smem(rows), smem(scales), pin(ph), pin(plo)

    got = swap(early)
    stream = [acc, pltpu.VMEM((DEPTH, GROUP, B, B), f32), pltpu.SemaphoreType.DMA((DEPTH, GROUP))]
    fb_shape = pltpu.VMEM((E * FACES, B, B), bf16)
    near, fb = call(
        load_kernel, "load", [SM] * 4 + [VM] * 3 + [ANY], [rows_of(16), fb_shape], stream,
        input_output_aliases={6: 1},
    )(me, faces, targets, bounds, pin(v), pin(pay), pin(fb), hbm(face_block))

    def exchange(wants_x, base, v, near, half, pay, got, fb, kernel=rest_kernel, more=(), outs=(), scratch=(acc,), **options):
        near, skip = call(
            bundle_kernel, "bundle", [SM, VM, VM, VM], [rows_of(16), rows_of(6)], input_output_aliases={3: 0},
        )(me, pin(got), pin(pay), pin(near))
        near, skip, half = near_swap(near), skip_shift(skip), half_swap(half)
        own, late, *others = call(
            kernel, "rest", [SM] * 4 + [VM] * 3 + [ANY if x is face_block else VM for x in more],
            [value, rows_of(18), *outs], scratch, **options,
        )(me, faces, targets, bounds, pin(v), pin(pay), pin(fb), *[hbm(x) if x is face_block else pin(x) for x in more])
        late = call(
            relay_kernel, "relay", [VM, VM, ANY, VM], [rows_of(18)], input_output_aliases={3: 0},
        )(pin(near), pin(skip), pin(half), pin(late))[0]
        if base is None:
            base, *others = others
        *x, u = call(
            functools.partial(gather_kernel, wants_x), "gather", [SM, SM] + [VM] * 7, [value] * (1 + wants_x), [total],
        )(me, donor, *map(pin, (base, own, near, skip, half)), ph, plo)
        return (x, u, swap(late)), *others

    def step(a, keep_x, wants_x, x, u, late, *rest):
        args = [pin(a)] if a is not None else []
        out, v, pay, early, half = call(
            lambda *refs: update_kernel(a is not None, keep_x, *refs), "update", [SM] * 4 + [VM] * (len(args) + len(x) + 3),
            [value] + sent, [total, value],
        )(me, donor, rows, scales, *args, *map(pin, x), pin(u), pin(late), ph)
        got = swap(early)
        near = call(
            near_kernel, "near", [SM] * 4 + [VM] * 3, [rows_of(16)], [acc],
        )(me, faces, targets, bounds, pin(v), pin(pay), fb)[0]
        if rest:
            kernel, more, outs = rest
            return out, *exchange(wants_x, None, v, near, half, pay, got, fb, kernel, (rhs, out, *more), [value, *outs])
        return out, *exchange(wants_x, out, v, near, half, pay, got, fb)

    sums, fb = exchange(
        False, rhs, v, near, half, pay, got, fb, rest_load_kernel, (face_block,), [fb_shape], stream,
        input_output_aliases={6: 2})
    fb = pin(fb)
    blocks = [pltpu.VMEM(BLOCK, bf16)] * 2
    a1, sums, dh, dl = step(None, False, True, *sums, rest_split_kernel, (diag_block,), blocks)
    _, sums = step(None, True, False, *sums)
    a2, sums = step(a1, False, True, *sums, rest_base_kernel, (dh, dl), [])
    _, sums = step(None, True, False, *sums)
    _, u, late = sums
    return pl.pallas_call(
        last_kernel, in_specs=[SM, SM] + [VM] * 4, out_specs=VM, out_shape=VALUE, scratch_shapes=[total],
        compiler_params=pltpu.CompilerParams(vmem_limit_bytes=20 * MIB), name="last",
    )(me, donor, pin(a2), pin(u), pin(late), ph)


def solution(mesh):
    dom = P("dom")
    return jax.shard_map(local, mesh=mesh, in_specs=(dom,) * 10, out_specs=dom, check_vma=False)
```

```python
import functools

import jax
import jax.numpy as jnp
from jax import lax
from jax.experimental import pallas as pl
from jax.experimental.pallas import tpu as pltpu
from jax.sharding import PartitionSpec as P

E = 8
R = 16
B = 320
FACES = 6
PAIRS = 16
N = 128
GROUP = 8
LIST = E * FACES + 2 * GROUP
AHEAD = 1
DEPTH = 3
MIB = 1024 * 1024
f32 = jnp.float32
bf16 = jnp.bfloat16

VM = pl.BlockSpec(memory_space=pltpu.VMEM)
SM = pl.BlockSpec(memory_space=pltpu.SMEM)
ANY = pl.BlockSpec(memory_space=pl.ANY)


def dot(a, b):
    return jnp.dot(a, b, preferred_element_type=f32)


def halves(x):
    high = x.astype(bf16)
    return high, (x - high.astype(f32)).astype(bf16)


def product(x, high, low):
    x_high, x_low = halves(x)
    both = dot(jnp.concatenate([x_high, x_low], axis=0), high)
    return both[:R] + both[R:] + dot(x_high, low)


def late_product(x, high):
    x_high, x_low = halves(x)
    both = dot(jnp.concatenate([x_high, x_low], axis=0), high)
    return both[:R] + both[R:]


def pair(k):
    return pl.ds(2 * k, 2)


def fill_tables(me, nbr, recv, dev, weight, count, faces, targets, bounds, rows, scales):
    core = lax.bitwise_and(me, 1)
    near_side = jnp.where(core == 0, 0, 2)
    for i in range(LIST):
        faces[i] = 0
        targets[i] = 2 * E
    kinds = []
    total = jnp.int32(0)
    for e in range(E):
        for f in range(FACES):
            n = nbr[e, f]
            side = lax.bitwise_and(lax.shift_right_logical(n, 3) - me + 129, 127)
            near = side == near_side
            row = lax.bitwise_and(n, 7)
            kinds.append((near, jnp.where(near | (side == 1), row, row + E)))
            total = total + near.astype(jnp.int32)
    groups = lax.div(total + GROUP - 1, GROUP)
    bounds[0] = groups
    bounds[1] = groups + lax.div(E * FACES - total + GROUP - 1, GROUP)
    first, second = jnp.int32(0), groups * GROUP
    for i, (near, row) in enumerate(kinds):
        at = jnp.where(near, first, second)
        faces[at] = i
        targets[at] = row
        step = near.astype(jnp.int32)
        first, second = first + step, second + 1 - step
    counts = [jnp.int32(0)] * 8
    for p in range(PAIRS):
        distance = lax.bitwise_and(dev[p] - me + 128, 127)
        bucket = jnp.where(distance <= 4, distance + 3, distance - 124)
        bucket = jnp.where(distance == 64, 7, bucket)
        position = jnp.int32(0)
        for k in range(8):
            hit = (bucket == k).astype(jnp.int32)
            position = position + hit * counts[k]
            counts[k] = counts[k] + hit
        rows[bucket * 2 + position] = recv[p]
        scales[bucket * 2 + position] = jnp.where(p < count[0], weight[p], f32(0.0))


def emit_pairs(core, v, rows, scales, pay, early, half):
    for slot in range(PAIRS):
        pay[slot] = (scales[slot] * v[rows[slot]]).astype(bf16)
    half[...] = pay[14:16]
    for j, (k0, k1) in enumerate(((5, 1), (6, 2), (0, 6), (1, 6))):
        early[2 * j : 2 * j + 2] = pay[pair(jnp.where(core == 0, k0, k1))]
    early[8:10] = pay[pair(jnp.where(core == 0, 4, 3))]


def add_faces(low, high, v, fb, faces, targets, acc):
    acc[...] = jnp.zeros_like(acc)

    def group(g, carry):
        terms = []
        for j in range(GROUP):
            face = faces[g * GROUP + j]
            terms.append(dot(v[lax.div(face, FACES)], fb[face]))
        for j in range(GROUP):
            acc[targets[g * GROUP + j]] += terms[j]
        return carry

    lax.fori_loop(low, high, group, 0)


def finish_near(core, acc, pay, near):
    near[0:E] = acc[0:E].astype(bf16)
    near[8:10] = pay[pair(jnp.where(core == 0, 3, 4))]
    near[12:14] = pay[pair(jnp.where(core == 0, 2, 5))]


def start_kernel(me, nbr, recv, dev, weight, count, rhs, precond, face,
                 faces, targets, bounds, rows, scales, ph, plo, fb, v_out, pay, early, half,
                 pbuf, fbuf, v, psem, fsem):
    def fetch(e):
        return pltpu.make_async_copy(precond.at[e], pbuf.at[e], psem.at[e])

    def fetch_face(e):
        return pltpu.make_async_copy(face.at[e], fbuf.at[e], fsem.at[e])

    for e in range(E):
        fetch(e).start()
    for e in range(AHEAD):
        fetch_face(e).start()
    fill_tables(me[0], nbr, recv, dev, weight, count, faces, targets, bounds, rows, scales)
    for e in range(E):
        fetch(e).wait()
        high, low = halves(pbuf[e])
        ph[e] = high
        plo[e] = low
        v[e] = product(rhs[e], high, low)
        v_out[e] = v[e].astype(bf16)
    emit_pairs(lax.bitwise_and(me[0], 1), v, rows, scales, pay, early, half)
    for e in range(AHEAD):
        fetch_face(e).wait()
        for f in range(FACES):
            fb[e * FACES + f] = fbuf[e, f].astype(bf16)


def add_streamed(low, high, v, face, fb, faces, targets, acc, fbuf, sems):
    acc[...] = jnp.zeros_like(acc)

    def each(g, act):
        slot = lax.rem(g - low, DEPTH)
        for j in range(GROUP):
            i = g * GROUP + j
            block = faces[i]

            @pl.when((targets[i] < 2 * E) & (block >= AHEAD * FACES))
            def _():
                source = face.at[lax.div(block, FACES), lax.rem(block, FACES)]
                act(block, fbuf.at[slot, j], pltpu.make_async_copy(source, fbuf.at[slot, j], sems.at[slot, j]))

    def start(block, held, copy):
        copy.start()

    def settle(block, held, copy):
        copy.wait()
        fb[block] = held[...].astype(bf16)

    for ahead in range(DEPTH):
        @pl.when(low + ahead < high)
        def _():
            each(low + ahead, start)

    def group(g, carry):
        each(g, settle)

        @pl.when(g + DEPTH < high)
        def _():
            each(g + DEPTH, start)

        terms = []
        for j in range(GROUP):
            block = faces[g * GROUP + j]
            terms.append(dot(v[lax.div(block, FACES)], fb[block]))
        for j in range(GROUP):
            acc[targets[g * GROUP + j]] += terms[j]
        return carry

    lax.fori_loop(low, high, group, 0)


def load_kernel(me, faces, targets, bounds, v, pay, fb_in, face, near, fb, acc, fbuf, sems):
    add_streamed(0, bounds[0], v, face, fb, faces, targets, acc, fbuf, sems)
    finish_near(lax.bitwise_and(me[0], 1), acc, pay, near)


def near_kernel(me, faces, targets, bounds, v, pay, fb, near, acc):
    add_faces(0, bounds[0], v, fb, faces, targets, acc)
    finish_near(lax.bitwise_and(me[0], 1), acc, pay, near)


def rest_load_kernel(me, faces, targets, bounds, v, pay, fb_in, face, own, late, fb, acc, fbuf, sems):
    add_streamed(bounds[0], bounds[1], v, face, fb, faces, targets, acc, fbuf, sems)
    finish_rest(lax.bitwise_and(me[0], 1), acc, pay, own, late)


def rest_split_kernel(me, faces, targets, bounds, v, pay, fb, rhs, a, diag, own, late, base, dh, dl, acc):
    rest_kernel(me, faces, targets, bounds, v, pay, fb, own, late, acc)
    for e in range(E):
        dh[e], dl[e] = halves(diag[e])
        base[e] = rhs[e] - product(a[e], dh[e], dl[e])


def rest_base_kernel(me, faces, targets, bounds, v, pay, fb, rhs, a, dh, dl, own, late, base, acc):
    rest_kernel(me, faces, targets, bounds, v, pay, fb, own, late, acc)
    for e in range(E):
        base[e] = rhs[e] - product(a[e], dh[e], dl[e])


def finish_rest(core, acc, pay, own, late):
    own[...] = acc[0:E]
    late[8:16] = acc[E : 2 * E].astype(bf16)


def rest_kernel(me, faces, targets, bounds, v, pay, fb, own, late, acc):
    add_faces(bounds[0], bounds[1], v, fb, faces, targets, acc)
    finish_rest(lax.bitwise_and(me[0], 1), acc, pay, own, late)


def bundle_kernel(me, got, pay, near_in, near, skip):
    core = lax.bitwise_and(me[0], 1)
    near[10:12] = got[pair(jnp.where(core == 0, 1, 0))]
    near[14:16] = got[pair(jnp.where(core == 0, 0, 1))]
    skip[0:2] = jnp.where(core == 0, got[4:6], pay[0:2])
    skip[2:4] = got[6:8]
    skip[4:6] = got[4:6]


def take(total, donor, k, row, live=None):
    for c in range(2):
        target = donor[2 * k + c]
        if live is not None:
            target = jnp.where(live, target, E)
        total[target] -= row[c].astype(f32)


def relay_kernel(near, skip, after, late_in, late):
    late[0:4] = near[12:16]
    late[4:8] = skip[0:4]


def gather_kernel(keep_x, me, donor, base, own, near, skip, half, got, ph, plo, *refs):
    *x_out, u_out, total = refs
    core = lax.bitwise_and(me[0], 1)
    total[0:E] = own[...] + near[0:E].astype(f32)
    total[E] = jnp.zeros((R, B), f32)
    take(total, donor, jnp.where(core == 0, 4, 3), near[8:10])
    take(total, donor, jnp.where(core == 0, 5, 2), near[10:12])
    take(total, donor, 7, half[...])
    take(total, donor, jnp.where(core == 0, 3, 4), got[8:10])
    take(total, donor, 0, skip[4:6], core == 0)
    for e in range(E):
        x = base[e] - total[e]
        if keep_x:
            x_out[0][e] = x
        u_out[e] = product(x, ph[e], plo[e])


def settle(core, donor, late, total):
    total[0:E] = late[8:16].astype(f32)
    total[E] = jnp.zeros((R, B), f32)
    take(total, donor, jnp.where(core == 0, 2, 5), late[0:2])
    take(total, donor, jnp.where(core == 0, 1, 6), late[2:4])
    take(total, donor, jnp.where(core == 0, 6, 0), late[4:6])
    take(total, donor, 1, late[6:8], core == 1)


def update_kernel(with_sum, keep_x, me, donor, rows, scales, *refs):
    if with_sum:
        a_in, *refs = refs
    if keep_x:
        x, *refs = refs
    u_in, late, ph, out, v_out, pay, early, half, total, v = refs
    core = lax.bitwise_and(me[0], 1)
    settle(core, donor, late, total)
    for e in range(E):
        u = u_in[e] - late_product(total[e], ph[e])
        if with_sum:
            u = u + a_in[e]
        v[e] = u
        v_out[e] = u.astype(bf16)
        out[e] = x[e] - total[e] if keep_x else u
    emit_pairs(core, v, rows, scales, pay, early, half)


def last_kernel(me, donor, a_in, u_in, late, ph, out, total):
    settle(lax.bitwise_and(me[0], 1), donor, late, total)
    for e in range(E):
        out[e] = a_in[e] + (u_in[e] - late_product(total[e], ph[e]))


VALUE = jax.ShapeDtypeStruct((E, R, B), f32)
BLOCK = (E, B, B)


def rows_of(count):
    return pltpu.VMEM((count, R, B), bf16)


def call(kernel, name, ins, outs, scratch=(), **options):
    return pl.pallas_call(
        kernel,
        in_specs=ins,
        out_specs=[SM if o.memory_space == pltpu.SMEM else VM for o in outs],
        out_shape=outs,
        scratch_shapes=scratch,
        compiler_params=pltpu.CompilerParams(vmem_limit_bytes=20 * MIB),
        name=name,
        **options,
    )


def pin(x, space=pltpu.VMEM):
    return pltpu.with_memory_space_constraint(x, space)


def swap(x):
    return lax.ppermute(x, "dom", [(s, s ^ 1) for s in range(N)])


def near_swap(x):
    return lax.ppermute(x, "dom", [(s, (s + (1 if s % 2 else -1)) % N) for s in range(N)])


def skip_shift(x):
    return lax.ppermute(x, "dom", [(s, (s + (-5 if s % 2 else 5)) % N) for s in range(N)])


def half_swap(x):
    return lax.ppermute(x, "dom", [(s, s ^ 64) for s in range(N)])


def local(rhs, diag_block, precond, face_block, face_nbr, pair_recv_elem, pair_donor_dev,
          pair_donor_elem, pair_weight, fringe_count):
    me = lax.axis_index("dom").astype(jnp.int32).reshape(1)
    donor = pair_donor_elem
    value = pltpu.VMEM((E, R, B), f32)
    total = pltpu.VMEM((E + 1, R, B), f32)
    acc = pltpu.VMEM((2 * E + 1, R, B), f32)
    sent = [rows_of(E), rows_of(PAIRS), rows_of(10), rows_of(2)]
    hbm = lambda x: pin(x, pltpu.HBM)
    smem = lambda x: pin(x, pltpu.SMEM)
    table = lambda n, dtype=jnp.int32: pltpu.SMEM((n,), dtype)

    faces, targets, bounds, rows, scales, ph, plo, fb, v, pay, early, half = call(
        start_kernel, "start", [SM] * 6 + [VM, ANY, ANY],
        [table(LIST), table(LIST), table(2), table(PAIRS), table(PAIRS, f32),
         pltpu.VMEM(BLOCK, bf16), pltpu.VMEM(BLOCK, bf16), pltpu.VMEM((E * FACES, B, B), bf16)] + sent,
        [pltpu.VMEM(BLOCK, f32), pltpu.VMEM((AHEAD, FACES, B, B), f32), value,
         pltpu.SemaphoreType.DMA((E,)), pltpu.SemaphoreType.DMA((AHEAD,))],
    )(me, hbm(face_nbr), hbm(pair_recv_elem), hbm(pair_donor_dev.reshape(-1)), hbm(pair_weight), fringe_count,
      hbm(rhs), hbm(precond), hbm(face_block))
    faces, targets, bounds = smem(faces), smem(targets), smem(bounds)
    rows, scales, ph, plo = smem(rows), smem(scales), pin(ph), pin(plo)

    got = swap(early)
    stream = [acc, pltpu.VMEM((DEPTH, GROUP, B, B), f32), pltpu.SemaphoreType.DMA((DEPTH, GROUP))]
    fb_shape = pltpu.VMEM((E * FACES, B, B), bf16)
    near, fb = call(
        load_kernel, "load", [SM] * 4 + [VM] * 3 + [ANY], [rows_of(16), fb_shape], stream,
        input_output_aliases={6: 1},
    )(me, faces, targets, bounds, pin(v), pin(pay), pin(fb), hbm(face_block))

    def exchange(wants_x, base, v, near, half, pay, got, fb, kernel=rest_kernel, more=(), outs=(), scratch=(acc,), **options):
        near, skip = call(
            bundle_kernel, "bundle", [SM, VM, VM, VM], [rows_of(16), rows_of(6)], input_output_aliases={3: 0},
        )(me, pin(got), pin(pay), pin(near))
        near, skip, half = near_swap(near), skip_shift(skip), half_swap(half)
        own, late, *others = call(
            kernel, "rest", [SM] * 4 + [VM] * 3 + [ANY if x is face_block else VM for x in more],
            [value, rows_of(16), *outs], scratch, **options,
        )(me, faces, targets, bounds, pin(v), pin(pay), pin(fb), *[hbm(x) if x is face_block else pin(x) for x in more])
        late = call(
            relay_kernel, "relay", [VM, VM, ANY, VM], [rows_of(16)], input_output_aliases={3: 0},
        )(pin(near), pin(skip), pin(half), pin(late))[0]
        if base is None:
            base, *others = others
        *x, u = call(
            functools.partial(gather_kernel, wants_x), "gather", [SM, SM] + [VM] * 8, [value] * (1 + wants_x), [total],
        )(me, donor, *map(pin, (base, own, near, skip, half, got)), ph, plo)
        return (x, u, swap(late)), *others

    def step(a, keep_x, wants_x, x, u, late, *rest):
        args = [pin(a)] if a is not None else []
        out, v, pay, early, half = call(
            lambda *refs: update_kernel(a is not None, keep_x, *refs), "update", [SM] * 4 + [VM] * (len(args) + len(x) + 3),
            [value] + sent, [total, value],
        )(me, donor, rows, scales, *args, *map(pin, x), pin(u), pin(late), ph)
        got = swap(early)
        near = call(
            near_kernel, "near", [SM] * 4 + [VM] * 3, [rows_of(16)], [acc],
        )(me, faces, targets, bounds, pin(v), pin(pay), fb)[0]
        if rest:
            kernel, more, outs = rest
            return out, *exchange(wants_x, None, v, near, half, pay, got, fb, kernel, (rhs, out, *more), [value, *outs])
        return out, *exchange(wants_x, out, v, near, half, pay, got, fb)

    sums, fb = exchange(
        False, rhs, v, near, half, pay, got, fb, rest_load_kernel, (face_block,), [fb_shape], stream,
        input_output_aliases={6: 2})
    fb = pin(fb)
    blocks = [pltpu.VMEM(BLOCK, bf16)] * 2
    a1, sums, dh, dl = step(None, False, True, *sums, rest_split_kernel, (diag_block,), blocks)
    _, sums = step(None, True, False, *sums)
    a2, sums = step(a1, False, True, *sums, rest_base_kernel, (dh, dl), [])
    _, sums = step(None, True, False, *sums)
    _, u, late = sums
    return pl.pallas_call(
        last_kernel, in_specs=[SM, SM] + [VM] * 4, out_specs=VM, out_shape=VALUE, scratch_shapes=[total],
        compiler_params=pltpu.CompilerParams(vmem_limit_bytes=20 * MIB), name="last",
    )(me, donor, pin(a2), pin(u), pin(late), ph)


def solution(mesh):
    dom = P("dom")
    return jax.shard_map(local, mesh=mesh, in_specs=(dom,) * 10, out_specs=dom, check_vma=False)
```
